128 devices in a mesh: seq: 16 (over x, z_hi, core), head: 4 (over y), section: 2 (over z_lo).
Axes of the slice: x: 4, y: 4, z: 4 (z_hi: 2, z_lo: 2; z = z_hi * 2 + z_lo), core: 2. Of those that a mesh axis runs over, the one named last changes fastest.
Arguments:
- prefill_queries: bfloat16 [2, 1024, 8192], P(None, 'seq', ('head', 'section')), as said below
- span_kv: bfloat16 [2, 1024, 8, 256], P(None, 'seq', ('head', 'section')), as said below
- prefix_cache: bfloat16 [2, 32768, 8, 256], P(None, 'seq', ('head', 'section')), may hold values from -5 to 5
- span_offsets: int32 [2], replicated, may hold values from 0 to 32768, as said below
- prompt_lengths: int32 [2], replicated, may hold values from 1 to 33792, as said below
- decode_owner: int32 [2], replicated, may hold values from 0 to 15
- out_weight: bfloat16 [8192, 5120], P(('head', 'section')), may hold values from -0.0625 to 0.0625
- step_queries: bfloat16 [4, 256, 8192], P(None, 'seq', ('head', 'section')), as said below
- step_kv: bfloat16 [4, 256, 8, 256], P(None, 'seq', ('head', 'section')), as said below
- decode_cache: bfloat16 [256, 1024, 8, 256], P('seq', None, ('head', 'section')), may hold values from -5 to 5
- contexts: int32 [256], P('seq'), may hold values from 1 to 1020, as said below
Outputs:
- prefill_out: bfloat16 [2, 1024, 5120], P(None, 'seq', ('head', 'section'))
- landed: bfloat16 [32, 1024, 8, 256], P('seq', None, ('head', 'section'))
- decode_out: bfloat16 [4, 256, 5120], P(None, 'seq', ('head', 'section'))
The draws below stay inside these ranges and needn't reach their ends.
Inputs may be any that keep to these rules, and one draw needn't show every extreme that they name: `span_offsets`: one prompt has offset 32768. `prompt_lengths`: each length exceeds its prompt's offset by 1 to 1024; the prompt with offset 32768 has length 33792. `contexts`: some request has 1020 positions in use. `prefill_queries`: rotated queries. `span_kv`: rotated keys and values. `step_queries`: rotated queries. `step_kv`: rotated keys and values.
All inputs are finite; a program needn't handle non-finite values.
Results may differ from the reference program's by a relative error of at most 0.013.
Values may be sent and summed in bfloat16 or wider, within the bound.
A program may use at most 384 MiB of HBM per device.

```python
import math
import jax
import jax.numpy as jnp
from jax import lax

D = 5120
QH = 64
KVH = 8
HD = 128
SEQS = 2
CH = 1024
CAP = 1024
STEPS = 4
PRE = 32768
BATCH = 256
N_SEQ = 16


def span_parts(key):
    key_rows = jax.random.truncated_normal(jax.random.fold_in(key, 11), -5.0, 5.0, (SEQS, CH, KVH, HD), jnp.float32)
    return key_rows


def step_parts(key):
    key_rows = jax.random.truncated_normal(jax.random.fold_in(key, 13), -5.0, 5.0, (STEPS, BATCH, KVH, HD), jnp.float32)
    return key_rows


def prompt_parts(key):
    chosen = jax.random.randint(jax.random.fold_in(key, 21), (), 0, SEQS)
    offsets = jax.random.randint(jax.random.fold_in(key, 22), (SEQS,), 0, PRE)
    fill_counts = jax.random.randint(jax.random.fold_in(key, 23), (SEQS,), 1, CH + 1)
    picked = jnp.arange(SEQS) == chosen
    offsets = jnp.where(picked, PRE, offsets)
    fill_counts = jnp.where(picked, CH, fill_counts)
    return (offsets.astype(jnp.int32), (offsets + fill_counts).astype(jnp.int32))


def draw_span_offsets(key, part):
    return prompt_parts(key)[0]


def draw_prompt_lengths(key, part):
    return prompt_parts(key)[1]


def draw_prefill_queries(key, part):
    key = jax.random.fold_in(key, 1)
    base_draw = 2.5 * jax.random.truncated_normal(key, -5.0, 5.0, (SEQS, CH, KVH, QH // KVH, HD), jnp.float32)
    return base_draw.reshape(SEQS, CH, QH * HD).astype(jnp.bfloat16)


def draw_span_kv(key, part):
    key_rows = span_parts(key)
    key = jax.random.fold_in(key, 2)
    value_rows = jax.random.truncated_normal(key, -5.0, 5.0, (SEQS, CH, KVH, HD), jnp.float32)
    return jnp.concatenate([key_rows, value_rows], axis=-1).astype(jnp.bfloat16)


def draw_step_queries(key, part):
    key = jax.random.fold_in(key, 3)
    base_draw = 2.5 * jax.random.truncated_normal(key, -5.0, 5.0, (STEPS, BATCH, KVH, QH // KVH, HD), jnp.float32)
    return base_draw.reshape(STEPS, BATCH, QH * HD).astype(jnp.bfloat16)


def draw_step_kv(key, part):
    key_rows = step_parts(key)
    key = jax.random.fold_in(key, 4)
    value_rows = jax.random.truncated_normal(key, -5.0, 5.0, (STEPS, BATCH, KVH, HD), jnp.float32)
    return jnp.concatenate([key_rows, value_rows], axis=-1).astype(jnp.bfloat16)


def draw_contexts(key, part):
    key = jax.random.fold_in(key, 5)
    chosen = jax.random.randint(jax.random.fold_in(key, 1), (), 0, BATCH)
    context_draw = jax.random.randint(jax.random.fold_in(key, 2), (BATCH,), 1, CAP - STEPS + 1)
    context_draw = jnp.where(jnp.arange(BATCH) == chosen, CAP - STEPS, context_draw)
    return context_draw.astype(jnp.int32)


def block_scale(stream_key, extent, split, least, top_value):
    def one(position, shards_of):
        steps = jax.random.uniform(jax.random.fold_in(jax.random.fold_in(stream_key, 6), position), (shards_of,), jnp.float32, least / len(split), top_value / len(split))
        return jnp.repeat(jnp.exp(steps), extent[position] // shards_of).reshape((-1,) + (1,) * (len(extent) - position - 1))

    level = one(*split[0])
    for cut in split[1:]:
        level = level * one(*cut)
    return level


def scatter_about(own_key, dims, spread, reach, split=(), held_as=jnp.bfloat16):
    result = spread * jax.random.normal(own_key, dims, jnp.float32)
    if split:
        result = result * block_scale(own_key, dims, split, -0.22, 0.18)
    return jnp.clip(result, -reach, reach).astype(held_as)


def setup_inputs(seed: int = 0) -> dict:
    key_of = jax.random.split(jax.random.key(seed), 12)
    return {
        "prefill_queries": draw_prefill_queries(jax.random.fold_in(key_of[11], 71), 0),
        "span_kv": draw_span_kv(jax.random.fold_in(key_of[11], 71), 0),
        "prefix_cache": scatter_about(key_of[2], (SEQS, PRE, KVH, 2 * HD), 1.0, 5.0, ((1, 16), (2, 8))),
        "span_offsets": draw_span_offsets(jax.random.fold_in(key_of[11], 71), 0),
        "prompt_lengths": draw_prompt_lengths(jax.random.fold_in(key_of[11], 71), 0),
        "decode_owner": jax.random.randint(key_of[5], (SEQS,), 0, N_SEQ).astype(jnp.int32),
        "out_weight": scatter_about(key_of[6], (QH * HD, D), (QH * HD) ** -0.5, 0.0625, ((0, 8),)),
        "step_queries": draw_step_queries(jax.random.fold_in(key_of[11], 71), 0),
        "step_kv": draw_step_kv(jax.random.fold_in(key_of[11], 71), 0),
        "decode_cache": scatter_about(key_of[9], (BATCH, CAP, KVH, 2 * HD), 1.0, 5.0, ((0, 16), (2, 8))),
        "contexts": draw_contexts(jax.random.fold_in(key_of[11], 71), 0),
    }


NEGATIVE_FILL = -1e30


def softmax_mix(scores, visible, values):
    scores = jnp.where(visible, scores, NEGATIVE_FILL)
    row_max = jnp.max(scores, axis=-1, keepdims=True)
    weights = jnp.where(visible, jnp.exp(scores - row_max), 0.0)
    denominator = jnp.sum(weights, axis=-1, keepdims=True)
    rounded = weights.astype(jnp.bfloat16).astype(jnp.float32)
    return rounded, denominator


def prefill_request(queries, span_rows, prefix, offset, length):
    fill_count = length - offset
    stacked = jnp.concatenate([prefix, span_rows], axis=0)
    positions = jnp.arange(PRE + CH, dtype=jnp.int32)
    block_rows = math.gcd(CH, 256)
    starts = jnp.arange(CH // block_rows, dtype=jnp.int32) * block_rows
    grouped = queries.reshape(CH, KVH, QH // KVH, HD)
    score_scale = HD ** -0.5

    def per_head(head_index):
        key_part = stacked[:, head_index, :HD].astype(jnp.float32)
        value_part = stacked[:, head_index, HD:].astype(jnp.float32)
        head_queries = grouped[:, head_index]

        def per_block(first_row):
            query_block = lax.dynamic_slice_in_dim(head_queries, first_row, block_rows, 0).astype(jnp.float32)
            row_ids = first_row + jnp.arange(block_rows, dtype=jnp.int32)
            span_pos = positions - PRE
            visible = jnp.where(positions[None, :] < PRE, positions[None, :] < offset,
                                (span_pos[None, :] <= row_ids[:, None]) & (span_pos[None, :] < fill_count))
            scores = jnp.einsum('qjd,nd->qjn', query_block, key_part) * score_scale
            rounded, denominator = softmax_mix(scores, visible[:, None, :], value_part)
            return jnp.einsum('qjn,nd->qjd', rounded, value_part) / denominator

        blocks_out = lax.map(per_block, starts)
        return blocks_out.reshape(CH, QH // KVH, HD)

    per_head_out = lax.map(per_head, jnp.arange(KVH, dtype=jnp.int32))
    per_head_out = jnp.moveaxis(per_head_out, 0, 1)
    row_live = jnp.arange(CH, dtype=jnp.int32) < fill_count
    per_head_out = jnp.where(row_live[:, None, None, None], per_head_out, 0.0)
    return per_head_out.astype(jnp.bfloat16).reshape(CH, QH * HD)


def decode_slot(inputs):
    queries, fresh, cache, context = inputs
    stacked = jnp.concatenate([cache, fresh], axis=0)
    positions = jnp.arange(CAP + STEPS, dtype=jnp.int32)
    step_ids = jnp.arange(STEPS, dtype=jnp.int32)
    visible = jnp.where(positions[None, :] < CAP, positions[None, :] < context,
                        (positions[None, :] - CAP) <= step_ids[:, None])
    grouped = queries.reshape(STEPS, KVH, QH // KVH, HD).astype(jnp.float32)
    key_part = stacked[..., :HD].astype(jnp.float32)
    value_part = stacked[..., HD:].astype(jnp.float32)
    scores = jnp.einsum('tgjd,ngd->tgjn', grouped, key_part) * (HD ** -0.5)
    rounded, denominator = softmax_mix(scores, visible[:, None, None, :], value_part)
    combined = jnp.einsum('tgjn,ngd->tgjd', rounded, value_part) / denominator
    return combined.astype(jnp.bfloat16).reshape(STEPS, QH * HD)


def reference(prefill_queries, span_kv, prefix_cache, span_offsets, prompt_lengths, decode_owner,
              out_weight, step_queries, step_kv, decode_cache, contexts):
    attended = jnp.stack([prefill_request(prefill_queries[index], span_kv[index], prefix_cache[index],
                                          span_offsets[index], prompt_lengths[index])
                          for index in range(SEQS)], axis=0)
    prefill_out = jnp.dot(attended.reshape(SEQS * CH, QH * HD), out_weight,
                          preferred_element_type=jnp.float32).astype(jnp.bfloat16).reshape(SEQS, CH, D)
    fill_counts = prompt_lengths - span_offsets
    token_keep = jnp.arange(CH, dtype=jnp.int32)[None, :] < fill_counts[:, None]
    owners = jnp.arange(N_SEQ, dtype=jnp.int32)[:, None] == decode_owner[None, :]
    landing_mask = owners[:, :, None] & token_keep[None]
    landed = jnp.where(landing_mask[..., None, None], span_kv[None], jnp.zeros((), span_kv.dtype))
    landed = landed.reshape(N_SEQ * SEQS, CH, KVH, 2 * HD)
    decoded_rows = lax.map(decode_slot, (jnp.moveaxis(step_queries, 1, 0), jnp.moveaxis(step_kv, 1, 0),
                                         decode_cache, contexts))
    decoded = jnp.moveaxis(decoded_rows, 0, 1).reshape(STEPS * BATCH, QH * HD)
    decode_out = jnp.dot(decoded, out_weight, preferred_element_type=jnp.float32)
    decode_out = decode_out.astype(jnp.bfloat16).reshape(STEPS, BATCH, D)
    return prefill_out, landed, decode_out
```

```python
import functools
import math

import jax
import jax.numpy as jnp
from jax import lax
from jax.experimental import pallas as pl
from jax.experimental.pallas import tpu as pltpu
from jax.sharding import PartitionSpec as P

MESH = pl.DeviceIdType.MESH
BF16 = jnp.bfloat16
F32 = jnp.float32
HIDDEN = -1e30
FLOOR = -1e29
LOG2E = math.log2(math.e)


def mul(a, b):
    return lax.dot_general(a, b, (((1,), (0,)), ((), ())), preferred_element_type=F32)


def mul_t(a, b):
    return lax.dot_general(a, b, (((1,), (1,)), ((), ())), preferred_element_type=F32)


def kernel(
    pq, skv, pre, w, dq, dstep, dcache, order, offs, fill, ctx,
    out_p, out_d,
    qg, kv, sk, wb, dcb, dqb, dsb, qhl, acc, mbuf, okeep, lkeep,
    zo_s, zl_s, zo_r, zl_r, xo_s, xl_s, xo_r, xl_r, att_s, att_r, decf,
    p1_s, p1_r, p1_own, p2_s, p2_r, p2_own,
    s_q, s_kv, s_w, s_dc, s_dq,
    sibq_s, sibq_r, sibkv_s, sibkv_r, sibsk_s, sibsk_r, siba_s, siba_r,
    agz_s, agz_r, agx_s, agx_r, rzo_s, rzo_r, rzl_s, rzl_r, rxo_s, rxo_r, rxl_s, rxl_r,
    o1_s, o1_r, o2_s, o2_r,
):
    seq, head, sec = lax.axis_index("seq"), lax.axis_index("head"), lax.axis_index("section")
    x, z, k = seq // 4, (seq // 2) % 2, seq % 2
    other = 1 - k
    chip = x * 2 + z
    scale = LOG2E / math.sqrt(128)

    def at_seq(xx, zz, kk):
        return (xx * 4 + zz * 2 + kk, head, sec)

    sibling = at_seq(x, z, other)
    zpeer = at_seq(x, 1 - z, k)

    def xpeer(d):
        return at_seq((x + d) % 4, z, k)

    def hpeer(n):
        return (seq, (head + n // 2) % 4, (sec + n) % 2)

    def remote(src, dst, ss, rs, dev):
        return pltpu.make_async_remote_copy(
            src_ref=src, dst_ref=dst, send_sem=ss, recv_sem=rs, device_id=dev, device_id_type=MESH
        )

    barrier = pltpu.get_barrier_semaphore()
    peers = [sibling, zpeer] + [xpeer(d) for d in (1, 2, 3)] + [hpeer(n) for n in range(1, 8)]
    for dev in peers:
        pl.semaphore_signal(barrier, inc=1, device_id=dev, device_id_type=MESH)
    pl.semaphore_wait(barrier, len(peers))

    def half(ref, r, kk):
        return ref.at[r, :, pl.ds(pl.multiple_of(kk * 512, 512), 512)]

    def own_q(r):
        return pltpu.make_async_copy(half(pq, r, k), qg.at[chip, r, k], s_q.at[r])

    def sib_q(r):
        return remote(half(pq, r, other), qg.at[chip, r, k], sibq_s.at[r], sibq_r.at[r], sibling)

    def got_sib_q(r):
        return remote(half(pq, r, other), qg.at[chip, r, other], sibq_s.at[r], sibq_r.at[r], sibling)

    def own_kv(r):
        return pltpu.make_async_copy(pre.at[r], kv.at[r, k], s_kv.at[r])

    def own_sk(r):
        return pltpu.make_async_copy(skv.at[r], sk.at[r, k], s_kv.at[2 + r])

    def sib_kv(r, kk):
        return remote(pre.at[r], kv.at[r, kk], sibkv_s.at[r], sibkv_r.at[r], sibling)

    def sib_sk(r, kk):
        return remote(skv.at[r], sk.at[r, kk], sibsk_s.at[r], sibsk_r.at[r], sibling)

    def dec_copy(b):
        return pltpu.make_async_copy(dcache.at[b], dcb.at[b], s_dc.at[b])

    def w_copy(p):
        return pltpu.make_async_copy(w.at[:, pl.ds(p * 640, 640)], wb.at[p], s_w.at[p])

    for r in range(2):
        sib_q(r).start()
        own_q(r).start()
    dq_copy = pltpu.make_async_copy(dq, dqb, s_dq.at[0])
    ds_copy = pltpu.make_async_copy(dstep, dsb, s_dq.at[1])
    dq_copy.start()
    ds_copy.start()
    for b in range(4):
        dec_copy(b).start()
    for r in range(2):
        sib_sk(r, k).start()
        sib_kv(r, k).start()
        own_sk(r).start()
        own_kv(r).start()
    for b in range(4, 16):
        dec_copy(b).start()
    for p in range(8):
        w_copy(p).start()

    def gz(j):
        return remote(qg.at[j], qg.at[j], agz_s.at[0], agz_r.at[0], zpeer)

    def gx(j, d, f):
        return remote(qg.at[j], qg.at[j], agx_s.at[d, f], agx_r.at[d, f], xpeer(4 - d))

    def task_chip(d, f):
        return ((x + d) % 4) * 2 + (z + f) % 2

    for r in range(2):
        own_q(r).wait()
        got_sib_q(r).wait_recv()
    gz(chip).start()
    for d in (1, 3, 2):
        gx(chip, d, 0).start()
    dq_copy.wait()
    ds_copy.wait()

    def decode_group(g, carry):
        row_step = lax.broadcasted_iota(jnp.int32, (32, 1024), 0) % 4
        key_id = lax.broadcasted_iota(jnp.int32, (32, 1024), 1)
        fresh = (key_id >= 1020) & (key_id - 1020 <= row_step)
        tail_rows = lax.broadcasted_iota(jnp.int32, (16, 256), 0) >= 12
        for e in range(4):
            b = g * 4 + e
            dec_copy(b).wait()
            tail = jnp.where(tail_rows, dsb[b].astype(F32), dcb[b, pl.ds(1008, 16), :].astype(F32))
            dcb[b, pl.ds(1008, 16), :] = tail.astype(BF16)
            s = mul_t(dqb[b], dcb[b, :, 0:128]) * scale
            seen = fresh | (key_id < ctx[b])
            s = jnp.where(seen, s, HIDDEN)
            m = jnp.max(s, axis=1, keepdims=True)
            pw = jnp.exp2(s - m)
            den = jnp.sum(pw, axis=1, keepdims=True)
            o = mul(pw.astype(BF16), dcb[b, :, 128:256]) / den
            for h in range(8):
                decf[b, :, h * 128 : h * 128 + 128] = o[h * 4 : h * 4 + 4, :]
        return carry

    lax.fori_loop(0, 2, decode_group, 0)
    gz(task_chip(0, 1)).wait_recv()
    for d in (1, 3, 2):
        gx(task_chip(0, 1), d, 1).start()
    lax.fori_loop(2, 4, decode_group, 0)

    for r in range(2):
        own_kv(r).wait()
        own_sk(r).wait()
        sib_kv(r, other).wait_recv()
        sib_sk(r, other).wait_recv()

    def rz_o(t):
        return remote(zo_s.at[t], zo_r.at[t], rzo_s.at[t], rzo_r.at[t], zpeer)

    def rz_l(t):
        return remote(zl_s.at[t], zl_r.at[t], rzl_s.at[t], rzl_r.at[t], zpeer)

    def rx_o(r, d):
        return remote(xo_s.at[r, d], xo_r.at[r, d], rxo_s.at[r, d], rxo_r.at[r, d], xpeer(d))

    def rx_l(r, d):
        return remote(xl_s.at[r, d], xl_r.at[r, d], rxl_s.at[r, d], rxl_r.at[r, d], xpeer(d))

    def spread(row):
        return jnp.transpose(jnp.broadcast_to(row, (128, 512)))

    def pack(col):
        return jnp.transpose(col)[0:8, :]

    def chain(t):
        r, d = t // 4, (t + 1) % 4
        rz_o(t).wait_recv()
        rz_l(t).wait_recv()
        l0, l1 = lkeep[...], spread(zl_r[t, 0:1, :])
        top = jnp.maximum(l0, l1)
        e0, e1 = jnp.exp2(l0 - top), jnp.exp2(l1 - top)
        den = e0 + e1
        o = ((okeep[...] * e0 + zo_r[t].astype(F32) * e1) / den).astype(BF16)
        lse = pack(top + jnp.log(den) * LOG2E)

        @pl.when(d == 0)
        def _():
            xo_r[r, 0] = o
            xl_r[r, 0] = lse

        @pl.when(d != 0)
        def _():
            xo_s[r, d] = o
            xl_s[r, d] = lse
            rx_o(r, d).start()
            rx_l(r, d).start()

    def sib_att(r):
        return remote(att_s.at[r, other], att_r.at[r, k], siba_s.at[r], siba_r.at[r], sibling)

    def got_sib_att(r):
        return remote(att_s.at[r, other], att_r.at[r, other], siba_s.at[r], siba_r.at[r], sibling)

    def settle(r):
        for d in (1, 2, 3):
            rx_o(r, d).wait_recv()
            rx_l(r, d).wait_recv()
        ls = [spread(xl_r[r, d, 0:1, :]) for d in range(4)]
        top = functools.reduce(jnp.maximum, ls)
        es = [jnp.exp2(v - top) for v in ls]
        den = functools.reduce(jnp.add, es)
        num = functools.reduce(jnp.add, [es[d] * xo_r[r, d].astype(F32) for d in range(4)])
        token = lax.broadcasted_iota(jnp.int32, (512, 128), 0) % 128 + chip * 128
        o = jnp.where(token < fill[order[r]], num / den, 0.0).astype(BF16)
        for h in range(4):
            for kk in range(2):
                att_s[r, kk, :, h * 128 : h * 128 + 128] = o[h * 128 + kk * 64 : h * 128 + kk * 64 + 64]
        sib_att(r).start()
        att_r[r, k] = att_s[r, k]

    def o1(n):
        return remote(p1_s.at[n], p1_r.at[n], o1_s.at[n], o1_r.at[n], hpeer(n))

    def o2(n):
        return remote(p2_s.at[n], p2_r.at[n], o2_s.at[n], o2_r.at[n], hpeer(n))

    def column_block(n):
        return ((head + n // 2) % 4) * 2 + (sec + n) % 2

    def project(lhs, n):
        p = column_block(n)
        return mul(lhs[0], wb[p, 0:512, :]) + mul(lhs[1], wb[p, 512:1024, :])

    def project_first():
        for p in range(8):
            w_copy(p).wait()
        got_sib_att(0).wait_recv()
        dec = jnp.concatenate([decf[:, t, :] for t in range(4)], axis=0).astype(BF16)
        lhs = [
            jnp.concatenate([dec[:, h * 512 : h * 512 + 512], att_r[0, h]], axis=0) for h in range(2)
        ]

        def step(n, carry):
            p1_s[n] = project(lhs, n).astype(BF16)
            o1(n).start()
            return carry

        lax.fori_loop(1, 8, step, 0)
        p1_own[...] = project(lhs, 0)

    def project_second():
        got_sib_att(1).wait_recv()
        lhs = [att_r[1, h] for h in range(2)]

        def step(n, carry):
            p2_s[n] = project(lhs, n).astype(BF16)
            o2(n).start()
            return carry

        lax.fori_loop(1, 8, step, 0)
        p2_own[...] = project(lhs, 0)

    ones = jnp.ones((256, 128), BF16)

    def task(t, carry):
        r, d = t // 4, (t + 1) % 4
        prompt = order[r]

        @pl.when((r == 0) & (d != 0))
        def _():
            for f in range(2):
                gx(task_chip(d, f), d, f).wait_recv()

        for f in range(2):
            both = [qg[task_chip(d, f), r2].reshape(128, 512).astype(F32) for r2 in range(2)]
            src = jnp.where(prompt == 0, both[0], both[1]) * scale
            base = 512 * (1 - f)
            for h in range(4):
                part = src[:, h * 128 : h * 128 + 128]
                hi = part.astype(BF16)
                qhl[base + h * 128 : base + h * 128 + 128, 0:128] = hi
                qhl[base + h * 128 : base + h * 128 + 128, 128:256] = (part - hi.astype(F32)).astype(BF16)

        rows = sk[prompt].reshape(128, 256)
        q = qhl[...]
        s = mul_t(q, jnp.concatenate([rows[:, 0:128], rows[:, 0:128]], axis=1))
        row = lax.broadcasted_iota(jnp.int32, (1024, 128), 0)
        key = lax.broadcasted_iota(jnp.int32, (1024, 128), 1) + chip * 128
        token = row % 128 + 128 * jnp.where(row < 512, task_chip(d, 1), task_chip(d, 0))
        seen = (key <= token) & (key < fill[prompt])
        s = jnp.where(seen, s, HIDDEN)
        m = jnp.maximum(jnp.broadcast_to(jnp.max(s, axis=1, keepdims=True), (1024, 128)), FLOOR)
        total = mul(
            jnp.exp2(s - m).astype(BF16), jnp.concatenate([rows[:, 128:256], ones[0:128]], axis=1)
        )
        for e in range(16):
            src, n0 = e // 8, e % 8 * 256
            kb = kv[prompt, src, n0 : n0 + 256, 0:128]
            vb = kv[prompt, src, n0 : n0 + 256, 128:256]
            pos = lax.broadcasted_iota(jnp.int32, (1, 256), 1) + (chip * 4096 + src * 2048 + n0)
            bias = jnp.where(pos < offs[prompt], 0.0, HIDDEN)
            s = mul_t(q, jnp.concatenate([kb, kb], axis=1)) + bias
            mn = jnp.maximum(m, jnp.broadcast_to(jnp.max(s, axis=1, keepdims=True), (1024, 128)))
            pw = jnp.exp2(s - jnp.concatenate([mn, mn], axis=1)).astype(BF16)
            rescale = jnp.exp2(m - mn)
            total = total * jnp.concatenate([rescale, rescale], axis=1) + mul(
                pw, jnp.concatenate([vb, ones], axis=1)
            )
            m = mn
        den = jnp.maximum(total[:, 128:256], 1e-30)
        acc[...] = total[:, 0:128] / den
        mbuf[...] = m + jnp.log(den) * LOG2E

        @pl.when(t > 0)
        def _():
            chain(t - 1)

        zo_s[t] = acc[0:512].astype(BF16)
        zl_s[t] = pack(mbuf[0:512])
        rz_o(t).start()
        rz_l(t).start()
        okeep[...] = acc[512:1024]
        lkeep[...] = mbuf[512:1024]

        @pl.when(t == 4)
        def _():
            settle(0)

        @pl.when(t == 5)
        def _():
            project_first()

        return carry

    lax.fori_loop(0, 8, task, 0)
    chain(7)
    settle(1)
    project_second()

    total = p1_own[...]
    for n in range(1, 8):
        o1(n).wait_recv()
        total = total + p1_r[n].astype(F32)
    out_d[...] = total[0:64].astype(BF16)
    first = total[64:128].astype(BF16)
    total = p2_own[...]
    for n in range(1, 8):
        o2(n).wait_recv()
        total = total + p2_r[n].astype(F32)
    second = total.astype(BF16)
    straight = order[0] == 0
    out_p[0] = jnp.where(straight, first.astype(F32), second.astype(F32)).astype(BF16)
    out_p[1] = jnp.where(straight, second.astype(F32), first.astype(F32)).astype(BF16)

    gz(chip).wait_send()
    for d in (1, 2, 3):
        gx(chip, d, 0).wait_send()
        gx(chip, d, 1).wait_send()
    for r in range(2):
        sib_q(r).wait_send()
        sib_kv(r, k).wait_send()
        sib_sk(r, k).wait_send()
        sib_att(r).wait_send()
        for d in (1, 2, 3):
            rx_o(r, d).wait_send()
            rx_l(r, d).wait_send()
    for t in range(8):
        rz_o(t).wait_send()
        rz_l(t).wait_send()
    for n in range(1, 8):
        o1(n).wait_send()
        o2(n).wait_send()


def run_kernel(*operands):
    dma = pltpu.SemaphoreType.DMA
    scratch = [
        pltpu.VMEM((8, 2, 2, 64, 512), BF16),
        pltpu.VMEM((2, 2, 2048, 256), BF16),
        pltpu.VMEM((2, 2, 64, 256), BF16),
        pltpu.VMEM((8, 1024, 640), BF16),
        pltpu.VMEM((16, 1024, 256), BF16),
        pltpu.VMEM((16, 32, 128), BF16),
        pltpu.VMEM((16, 16, 256), BF16),
        pltpu.VMEM((1024, 256), BF16),
        pltpu.VMEM((1024, 128), F32),
        pltpu.VMEM((1024, 128), F32),
        pltpu.VMEM((512, 128), F32),
        pltpu.VMEM((512, 128), F32),
        pltpu.VMEM((8, 512, 128), BF16),
        pltpu.VMEM((8, 8, 512), F32),
        pltpu.VMEM((8, 512, 128), BF16),
        pltpu.VMEM((8, 8, 512), F32),
        pltpu.VMEM((2, 4, 512, 128), BF16),
        pltpu.VMEM((2, 4, 8, 512), F32),
        pltpu.VMEM((2, 4, 512, 128), BF16),
        pltpu.VMEM((2, 4, 8, 512), F32),
        pltpu.VMEM((2, 2, 64, 512), BF16),
        pltpu.VMEM((2, 2, 64, 512), BF16),
        pltpu.VMEM((16, 4, 1024), F32),
        pltpu.VMEM((8, 128, 640), BF16),
        pltpu.VMEM((8, 128, 640), BF16),
        pltpu.VMEM((128, 640), F32),
        pltpu.VMEM((8, 64, 640), BF16),
        pltpu.VMEM((8, 64, 640), BF16),
        pltpu.VMEM((64, 640), F32),
        dma((2,)), dma((4,)), dma((8,)), dma((16,)), dma((2,)),
        dma((2,)), dma((2,)), dma((2,)), dma((2,)), dma((2,)), dma((2,)), dma((2,)), dma((2,)),
        dma((1,)), dma((1,)), dma((4, 2)), dma((4, 2)),
        dma((8,)), dma((8,)), dma((8,)), dma((8,)),
        dma((2, 4)), dma((2, 4)), dma((2, 4)), dma((2, 4)),
        dma((8,)), dma((8,)), dma((8,)), dma((8,)),
    ]
    hbm = pl.BlockSpec(memory_space=pl.ANY)
    smem = pl.BlockSpec(memory_space=pltpu.SMEM)
    vmem = pl.BlockSpec(memory_space=pltpu.VMEM)
    return pl.pallas_call(
        kernel,
        out_shape=(
            jax.ShapeDtypeStruct((2, 64, 640), BF16),
            jax.ShapeDtypeStruct((64, 640), BF16),
        ),
        in_specs=[hbm] * 7 + [smem] * 4,
        out_specs=(vmem, vmem),
        scratch_shapes=scratch,
        compiler_params=pltpu.CompilerParams(
            collective_id=0, has_side_effects=True, vmem_limit_bytes=60 * 2**20
        ),
        cost_estimate=pl.CostEstimate(
            flops=40_000_000_000, bytes_accessed=24 * 2**20, transcendentals=36_000_000
        ),
        name="attend_and_project",
    )(*operands)


def shards(
    prefill_queries,
    span_kv,
    prefix_cache,
    span_offsets,
    prompt_lengths,
    decode_owner,
    out_weight,
    step_queries,
    step_kv,
    decode_cache,
    contexts,
):
    fill_counts = prompt_lengths - span_offsets
    first = (fill_counts[1] > fill_counts[0]).astype(jnp.int32)
    order = jnp.stack([first, 1 - first])
    dq = step_queries.reshape(4, 16, 8, 128).transpose(1, 2, 0, 3).reshape(16, 32, 128)
    dstep = jnp.pad(step_kv.reshape(4, 16, 256).transpose(1, 0, 2), ((0, 0), (12, 0), (0, 0)))
    prefill_out, decode_out = run_kernel(
        prefill_queries,
        span_kv.reshape(2, 64, 256),
        prefix_cache.reshape(2, 2048, 256),
        out_weight,
        dq,
        dstep,
        decode_cache.reshape(16, 1024, 256),
        order,
        span_offsets,
        fill_counts,
        contexts,
    )
    span_all = lax.all_gather(span_kv, "seq", axis=1, tiled=True)
    token_keep = (jnp.arange(1024, dtype=jnp.int32)[None, :] < fill_counts[:, None]) & (
        decode_owner == lax.axis_index("seq")
    )[:, None]
    landed = jnp.where(token_keep[:, :, None, None], span_all, jnp.zeros((), span_all.dtype))
    return (prefill_out, landed, decode_out.reshape(4, 16, 640))


def solution(mesh):
    placed = (
        P(None, "seq", ("head", "section")),
        P(None, "seq", ("head", "section"), None),
        P(None, "seq", ("head", "section"), None),
        P(),
        P(),
        P(),
        P(("head", "section"), None),
        P(None, "seq", ("head", "section")),
        P(None, "seq", ("head", "section"), None),
        P("seq", None, ("head", "section"), None),
        P("seq"),
    )
    return jax.shard_map(
        shards,
        mesh=mesh,
        in_specs=placed,
        out_specs=(
            P(None, "seq", ("head", "section")),
            P("seq", None, ("head", "section"), None),
            P(None, "seq", ("head", "section")),
        ),
        check_vma=False,
    )
```

```python
import functools
import math

import jax
import jax.numpy as jnp
from jax import lax
from jax.experimental import pallas as pl
from jax.experimental.pallas import tpu as pltpu
from jax.sharding import PartitionSpec as P

MESH = pl.DeviceIdType.MESH
BF16 = jnp.bfloat16
F32 = jnp.float32
HIDDEN = -1e30
FLOOR = -1e29
LOG2E = math.log2(math.e)


def mul(a, b):
    return lax.dot_general(a, b, (((1,), (0,)), ((), ())), preferred_element_type=F32)


def mul_t(a, b):
    return lax.dot_general(a, b, (((1,), (1,)), ((), ())), preferred_element_type=F32)


def kernel(
    pq, skv, pre, w, sq, stepkv, dcache, offs, lens, owner, ctx,
    out_p, out_l, out_d,
    pqv, qst, qg, kv, sk, wb, dcb, sqv, skvv, dqf, dsf, qhl, acc, mbuf, okeep, lkeep,
    zo_s, zl_s, zo_r, zl_r, xo_s, xl_s, xo_r, xl_r, att_s, att_r, decf,
    p_s, p_r, p_own, spg, lnd,
    s_q, s_kv, s_w, s_dc, s_dq,
    sibq_s, sibq_r, sibkv_s, sibkv_r, sibsk_s, sibsk_r, siba_s, siba_r,
    agz_s, agz_r, agx_s, agx_r, rzo_s, rzo_r, rzl_s, rzl_r, rxo_s, rxo_r, rxl_s, rxl_r,
    o_s, o_r, sp_s, sp_r, sps_s, sps_r, s_l,
):
    seq, head, sec = lax.axis_index("seq"), lax.axis_index("head"), lax.axis_index("section")
    x, z, k = seq // 4, (seq // 2) % 2, seq % 2
    other = 1 - k
    chip = x * 2 + z
    scale = LOG2E / math.sqrt(128)
    swapped = ((lens[1] - offs[1]) > (lens[0] - offs[0])).astype(jnp.int32)

    def prompt_of(phase):
        return jnp.where(phase == 0, swapped, 1 - swapped)

    def fill_of(prompt):
        return lens[prompt] - offs[prompt]

    def at_seq(xx, zz, kk):
        return (xx * 4 + zz * 2 + kk, head, sec)

    sibling = at_seq(x, z, other)
    zpeer = at_seq(x, 1 - z, k)

    def xpeer(d):
        return at_seq((x + d) % 4, z, k)

    def plane_peer(n):
        return at_seq((x + n // 2) % 4, (z + n) % 2, k)

    def hpeer(n):
        return (seq, (head + n // 2) % 4, (sec + n) % 2)

    def remote(src, dst, ss, rs, dev):
        return pltpu.make_async_remote_copy(
            src_ref=src, dst_ref=dst, send_sem=ss, recv_sem=rs, device_id=dev, device_id_type=MESH
        )

    barrier = pltpu.get_barrier_semaphore()
    peers = [sibling] + [plane_peer(n) for n in range(1, 8)] + [hpeer(n) for n in range(1, 8)]
    for dev in peers:
        pl.semaphore_signal(barrier, inc=1, device_id=dev, device_id_type=MESH)
    pl.semaphore_wait(barrier, len(peers))

    q_copy = pltpu.make_async_copy(pq, pqv, s_q.at[0])

    def sib_q(r):
        return remote(qst.at[r], qg.at[chip, r, k], sibq_s.at[r], sibq_r.at[r], sibling)

    def got_sib_q(r):
        return remote(qst.at[r], qg.at[chip, r, other], sibq_s.at[r], sibq_r.at[r], sibling)

    def own_kv(r):
        return pltpu.make_async_copy(pre.at[r], kv.at[r, k], s_kv.at[r])

    def own_sk(r):
        return pltpu.make_async_copy(skv.at[r], sk.at[r, k], s_kv.at[2 + r])

    def sib_kv(r, kk):
        return remote(pre.at[r], kv.at[r, kk], sibkv_s.at[r], sibkv_r.at[r], sibling)

    def sib_sk(r, kk):
        return remote(skv.at[r], sk.at[r, kk], sibsk_s.at[r], sibsk_r.at[r], sibling)

    def dec_copy(b):
        return pltpu.make_async_copy(dcache.at[b], dcb.at[b], s_dc.at[b])

    def w_copy(p):
        return pltpu.make_async_copy(w.at[:, pl.ds(p * 640, 640)], wb.at[p], s_w.at[p])

    q_copy.start()
    sq_copy = pltpu.make_async_copy(sq, sqv, s_dq.at[0])
    st_copy = pltpu.make_async_copy(stepkv, skvv, s_dq.at[1])
    sq_copy.start()
    st_copy.start()
    for b in range(4):
        dec_copy(b).start()
    q_copy.wait()
    for r in range(2):
        mine = jnp.where(prompt_of(r) == 0, pqv[0].astype(F32), pqv[1].astype(F32)).astype(BF16)
        left, right = mine[:, 0:512].astype(F32), mine[:, 512:1024].astype(F32)
        qg[chip, r, k] = jnp.where(k == 0, left, right).astype(BF16)
        qst[r] = jnp.where(k == 0, right, left).astype(BF16)
        sib_q(r).start()
    for r in range(2):
        sib_sk(r, k).start()
        sib_kv(r, k).start()
        own_sk(r).start()
        own_kv(r).start()
    for b in range(4, 16):
        dec_copy(b).start()
    for p in range(8):
        w_copy(p).start()

    def gz(j, r):
        return remote(qg.at[j, r], qg.at[j, r], agz_s.at[r], agz_r.at[r], zpeer)

    def gx(j, d, f, r):
        return remote(
            qg.at[j, r], qg.at[j, r], agx_s.at[d, f, r], agx_r.at[d, f, r], xpeer(4 - d)
        )

    def task_chip(d, f):
        return ((x + d) % 4) * 2 + (z + f) % 2

    got_sib_q(0).wait_recv()
    gz(chip, 0).start()
    gx(chip, 1, 0, 0).start()
    gx(chip, 3, 0, 0).start()
    got_sib_q(1).wait_recv()

    sq_copy.wait()
    st_copy.wait()
    for t in range(4):
        step_q = sqv[t].astype(F32)
        for h in range(8):
            dqf[:, h * 4 + t, :] = step_q[:, h * 128 : h * 128 + 128]
        dsf[:, 4 + t, :] = skvv[t].astype(F32)

    def decode_group(g, carry):
        row_step = lax.broadcasted_iota(jnp.int32, (32, 1024), 0) % 4
        key_id = lax.broadcasted_iota(jnp.int32, (32, 1024), 1)
        fresh = (key_id >= 1020) & (key_id - 1020 <= row_step)
        step_rows = lax.broadcasted_iota(jnp.int32, (8, 256), 0) >= 4
        for e in range(4):
            b = g * 4 + e
            dec_copy(b).wait()
            tail = dcb[b, pl.ds(1008, 16), :].astype(F32)
            tail = jnp.concatenate([tail[0:8], jnp.where(step_rows, dsf[b], tail[8:16])], axis=0)
            dcb[b, pl.ds(1008, 16), :] = tail.astype(BF16)
            s = mul_t(dqf[b].astype(BF16), dcb[b, :, 0:128]) * scale
            seen = fresh | (key_id < ctx[b])
            s = jnp.where(seen, s, HIDDEN)
            m = jnp.max(s, axis=1, keepdims=True)
            pw = jnp.exp2(s - m)
            den = jnp.sum(pw, axis=1, keepdims=True)
            o = mul(pw.astype(BF16), dcb[b, :, 128:256]) / den
            for h in range(8):
                decf[b, :, h * 128 : h * 128 + 128] = o[h * 4 : h * 4 + 4, :]
        return carry

    lax.fori_loop(0, 1, decode_group, 0)
    gz(task_chip(0, 1), 0).wait_recv()
    gx(task_chip(0, 1), 1, 1, 0).start()
    gx(task_chip(0, 1), 3, 1, 0).start()
    gx(chip, 2, 0, 0).start()
    gx(task_chip(0, 1), 2, 1, 0).start()
    lax.fori_loop(1, 3, decode_group, 0)
    gz(chip, 1).start()
    lax.fori_loop(3, 4, decode_group, 0)

    def rz_o(t):
        return remote(zo_s.at[t], zo_r.at[t], rzo_s.at[t], rzo_r.at[t], zpeer)

    def rz_l(t):
        return remote(zl_s.at[t], zl_r.at[t], rzl_s.at[t], rzl_r.at[t], zpeer)

    def rx_o(r, d):
        return remote(xo_s.at[r, d], xo_r.at[r, d], rxo_s.at[r, d], rxo_r.at[r, d], xpeer(d))

    def rx_l(r, d):
        return remote(xl_s.at[r, d], xl_r.at[r, d], rxl_s.at[r, d], rxl_r.at[r, d], xpeer(d))

    def spread(row):
        return jnp.transpose(jnp.broadcast_to(row, (128, 512)))

    def pack(col):
        return jnp.transpose(col)[0:8, :]

    def task_step(t):
        return (t + t // 4) % 4

    def chain(t):
        r, d = t // 4, task_step(t)
        rz_o(t).wait_recv()
        rz_l(t).wait_recv()
        l0, l1 = lkeep[...], spread(zl_r[t, 0:1, :])
        top = jnp.maximum(l0, l1)
        e0, e1 = jnp.exp2(l0 - top), jnp.exp2(l1 - top)
        den = e0 + e1
        o = ((okeep[...] * e0 + zo_r[t].astype(F32) * e1) / den).astype(BF16)
        lse = pack(top + jnp.log(den) * LOG2E)

        @pl.when(d == 0)
        def _():
            xo_r[r, 0] = o
            xl_r[r, 0] = lse

        @pl.when(d != 0)
        def _():
            xo_s[r, d] = o
            xl_s[r, d] = lse
            rx_o(r, d).start()
            rx_l(r, d).start()

    def sib_att(r):
        return remote(att_s.at[r, other], att_r.at[r, k], siba_s.at[r], siba_r.at[r], sibling)

    def got_sib_att(r):
        return remote(att_s.at[r, other], att_r.at[r, other], siba_s.at[r], siba_r.at[r], sibling)

    def settle(r):
        for d in (1, 2, 3):
            rx_o(r, d).wait_recv()
            rx_l(r, d).wait_recv()
        ls = [spread(xl_r[r, d, 0:1, :]) for d in range(4)]
        top = functools.reduce(jnp.maximum, ls)
        es = [jnp.exp2(v - top) for v in ls]
        den = functools.reduce(jnp.add, es)
        num = functools.reduce(jnp.add, [es[d] * xo_r[r, d].astype(F32) for d in range(4)])
        token = lax.broadcasted_iota(jnp.int32, (512, 128), 0) % 128 + chip * 128
        o = jnp.where(token < fill_of(prompt_of(r)), num / den, 0.0).astype(BF16)
        for h in range(4):
            for kk in range(2):
                att_s[r, kk, :, h * 128 : h * 128 + 128] = o[h * 128 + kk * 64 : h * 128 + kk * 64 + 64]
        sib_att(r).start()
        att_r[r, k] = att_s[r, k]

    def to_owner(stage, n):
        return remote(
            p_s.at[stage, n], p_r.at[stage, n], o_s.at[stage, n], o_r.at[stage, n], hpeer(n)
        )

    def column_block(n):
        return ((head + n // 2) % 4) * 2 + (sec + n) % 2

    def project(lhs, n):
        p = column_block(n)
        return mul(lhs[0], wb[p, 0:512, :]) + mul(lhs[1], wb[p, 512:1024, :])

    def project_stage(stage, lhs):
        def step(n, carry):
            p_s[stage, n] = project(lhs, n).astype(BF16)
            to_owner(stage, n).start()
            return carry

        lax.fori_loop(1, 8, step, 0)
        p_own[stage] = project(lhs, 0)

    def project_prompt(r):
        got_sib_att(r).wait_recv()
        project_stage(1 + r, [att_r[r, h] for h in range(2)])

    def span_out(n):
        return remote(sk.at[k], spg.at[k, chip], sp_s.at[n], sp_r.at[n], plane_peer(n))

    def span_in(n):
        source = ((x - n // 2) % 4) * 2 + (z + n) % 2
        return remote(sk.at[k], spg.at[k, source], sp_s.at[n], sp_r.at[n], plane_peer(n))

    def span_swap(r):
        return remote(spg.at[r], spg.at[r], sps_s.at[0], sps_r.at[0], sibling)

    def land_copy():
        return pltpu.make_async_copy(lnd, out_l, s_l.at[0])

    def land():
        span_swap(other).wait_recv()
        for r in range(2):
            token = lax.broadcasted_iota(jnp.int32, (1024, 256), 0)
            limit = jnp.where(owner[r] == seq, fill_of(r), 0)
            rows = spg[r].reshape(1024, 256).astype(F32)
            lnd[r] = jnp.where(token < limit, rows, 0.0).astype(BF16)
        land_copy().start()

    for p in range(8):
        w_copy(p).wait()
    dec = jnp.concatenate([decf[:, t, :] for t in range(4)], axis=0).astype(BF16)
    project_stage(0, [dec[:, h * 512 : h * 512 + 512] for h in range(2)])

    for r in range(2):
        own_kv(r).wait()
        own_sk(r).wait()
        sib_kv(r, other).wait_recv()
        sib_sk(r, other).wait_recv()

    ones = jnp.ones((256, 128), BF16)

    def load_queries(r, d):
        for f in range(2):
            src = qg[task_chip(d, f), r].reshape(128, 512).astype(F32) * scale
            base = 512 * (1 - f)
            for h in range(4):
                part = src[:, h * 128 : h * 128 + 128]
                hi = part.astype(BF16)
                qhl[base + h * 128 : base + h * 128 + 128, 0:128] = hi
                qhl[base + h * 128 : base + h * 128 + 128, 128:256] = (part - hi.astype(F32)).astype(BF16)

    def attend(prompt, d, lo, n):
        limit, seen_prefix = fill_of(prompt), offs[prompt]
        q = qhl[lo : lo + n, :]
        rows = sk[prompt].reshape(128, 256)
        s = mul_t(q, jnp.concatenate([rows[:, 0:128], rows[:, 0:128]], axis=1))
        row = lax.broadcasted_iota(jnp.int32, (n, 128), 0) + lo
        key = lax.broadcasted_iota(jnp.int32, (n, 128), 1) + chip * 128
        token = row % 128 + 128 * jnp.where(row < 512, task_chip(d, 1), task_chip(d, 0))
        seen = (key <= token) & (key < limit)
        s = jnp.where(seen, s, HIDDEN)
        m = jnp.maximum(jnp.broadcast_to(jnp.max(s, axis=1, keepdims=True), (n, 128)), FLOOR)
        total = mul(
            jnp.exp2(s - m).astype(BF16), jnp.concatenate([rows[:, 128:256], ones[0:128]], axis=1)
        )
        for e in range(16):
            src, n0 = e // 8, e % 8 * 256
            kb = kv[prompt, src, n0 : n0 + 256, 0:128]
            vb = kv[prompt, src, n0 : n0 + 256, 128:256]
            pos = lax.broadcasted_iota(jnp.int32, (1, 256), 1) + (chip * 4096 + src * 2048 + n0)
            bias = jnp.where(pos < seen_prefix, 0.0, HIDDEN)
            s = mul_t(q, jnp.concatenate([kb, kb], axis=1)) + bias
            mn = jnp.maximum(m, jnp.broadcast_to(jnp.max(s, axis=1, keepdims=True), (n, 128)))
            pw = jnp.exp2(s - jnp.concatenate([mn, mn], axis=1)).astype(BF16)
            rescale = jnp.exp2(m - mn)
            total = total * jnp.concatenate([rescale, rescale], axis=1) + mul(
                pw, jnp.concatenate([vb, ones], axis=1)
            )
            m = mn
        den = jnp.maximum(total[:, 128:256], 1e-30)
        acc[lo : lo + n, :] = total[:, 0:128] / den
        mbuf[lo : lo + n, :] = m + jnp.log(den) * LOG2E

    def send_z(t):
        zo_s[t] = acc[0:512].astype(BF16)
        zl_s[t] = pack(mbuf[0:512])
        rz_o(t).start()
        rz_l(t).start()

    def keep():
        okeep[...] = acc[512:1024]
        lkeep[...] = mbuf[512:1024]

    def await_queries(r, d):
        for f in range(2):
            gx(task_chip(d, f), d, f, r).wait_recv()

    def task(t, carry):
        r, d = t // 4, task_step(t)

        @pl.when(d != 0)
        def _():
            await_queries(r, d)

        load_queries(r, d)
        attend(prompt_of(r), d, 0, 1024)

        @pl.when(t > 0)
        def _():
            chain(t - 1)

        send_z(t)
        keep()

        @pl.when(t == 0)
        def _():
            gz(task_chip(0, 1), 1).wait_recv()
            for d2 in (1, 3, 2):
                gx(chip, d2, 0, 1).start()
                gx(task_chip(0, 1), d2, 1, 1).start()

        @pl.when(t == 2)
        def _():
            spg[k, chip] = sk[k]
            for n in range(1, 8):
                span_out(n).start()

        @pl.when(t == 4)
        def _():
            for n in range(1, 8):
                span_in(n).wait_recv()
            span_swap(k).start()

        @pl.when(t == 5)
        def _():
            settle(0)
            land()

        @pl.when(t == 6)
        def _():
            project_prompt(0)

        return carry

    lax.fori_loop(0, 7, task, 0)
    load_queries(1, 0)
    attend(prompt_of(1), 0, 0, 512)
    send_z(7)
    attend(prompt_of(1), 0, 512, 512)
    chain(6)
    keep()
    chain(7)
    settle(1)
    project_prompt(1)

    def gathered(stage):
        total = p_own[stage]
        for n in range(1, 8):
            to_owner(stage, n).wait_recv()
            total = total + p_r[stage, n].astype(F32)
        return total.astype(BF16)

    out_d[...] = gathered(0)
    first = gathered(1)
    second = gathered(2)
    straight = swapped == 0
    out_p[0] = jnp.where(straight, first.astype(F32), second.astype(F32)).astype(BF16)
    out_p[1] = jnp.where(straight, second.astype(F32), first.astype(F32)).astype(BF16)

    for r in range(2):
        gz(chip, r).wait_send()
        for d in (1, 2, 3):
            gx(chip, d, 0, r).wait_send()
            gx(task_chip(0, 1), d, 1, r).wait_send()
        sib_q(r).wait_send()
        sib_kv(r, k).wait_send()
        sib_sk(r, k).wait_send()
        sib_att(r).wait_send()
        for d in (1, 2, 3):
            rx_o(r, d).wait_send()
            rx_l(r, d).wait_send()
    for t in range(8):
        rz_o(t).wait_send()
        rz_l(t).wait_send()
    span_swap(k).wait_send()
    land_copy().wait()
    for n in range(1, 8):
        span_out(n).wait_send()
        for stage in range(3):
            to_owner(stage, n).wait_send()


def run_kernel(*operands):
    dma = pltpu.SemaphoreType.DMA
    scratch = [
        pltpu.VMEM((2, 64, 1024), BF16),
        pltpu.VMEM((2, 64, 512), BF16),
        pltpu.VMEM((8, 2, 2, 64, 512), BF16),
        pltpu.VMEM((2, 2, 2048, 256), BF16),
        pltpu.VMEM((2, 2, 64, 256), BF16),
        pltpu.VMEM((8, 1024, 640), BF16),
        pltpu.VMEM((16, 1024, 256), BF16),
        pltpu.VMEM((4, 16, 1024), BF16),
        pltpu.VMEM((4, 16, 256), BF16),
        pltpu.VMEM((16, 32, 128), F32),
        pltpu.VMEM((16, 8, 256), F32),
        pltpu.VMEM((1024, 256), BF16),
        pltpu.VMEM((1024, 128), F32),
        pltpu.VMEM((1024, 128), F32),
        pltpu.VMEM((512, 128), F32),
        pltpu.VMEM((512, 128), F32),
        pltpu.VMEM((8, 512, 128), BF16),
        pltpu.VMEM((8, 8, 512), F32),
        pltpu.VMEM((8, 512, 128), BF16),
        pltpu.VMEM((8, 8, 512), F32),
        pltpu.VMEM((2, 4, 512, 128), BF16),
        pltpu.VMEM((2, 4, 8, 512), F32),
        pltpu.VMEM((2, 4, 512, 128), BF16),
        pltpu.VMEM((2, 4, 8, 512), F32),
        pltpu.VMEM((2, 2, 64, 512), BF16),
        pltpu.VMEM((2, 2, 64, 512), BF16),
        pltpu.VMEM((16, 4, 1024), F32),
        pltpu.VMEM((3, 8, 64, 640), BF16),
        pltpu.VMEM((3, 8, 64, 640), BF16),
        pltpu.VMEM((3, 64, 640), F32),
        pltpu.VMEM((2, 8, 2, 64, 256), BF16),
        pltpu.VMEM((2, 1024, 256), BF16),
        dma((1,)), dma((4,)), dma((8,)), dma((16,)), dma((2,)),
        dma((2,)), dma((2,)), dma((2,)), dma((2,)), dma((2,)), dma((2,)), dma((2,)), dma((2,)),
        dma((2,)), dma((2,)), dma((4, 2, 2)), dma((4, 2, 2)),
        dma((8,)), dma((8,)), dma((8,)), dma((8,)),
        dma((2, 4)), dma((2, 4)), dma((2, 4)), dma((2, 4)),
        dma((3, 8)), dma((3, 8)), dma((8,)), dma((8,)), dma((1,)), dma((1,)), dma((1,)),
    ]
    hbm = pl.BlockSpec(memory_space=pl.ANY)
    smem = pl.BlockSpec(memory_space=pltpu.SMEM)
    vmem = pl.BlockSpec(memory_space=pltpu.VMEM)
    return pl.pallas_call(
        kernel,
        out_shape=(
            jax.ShapeDtypeStruct((2, 64, 640), BF16),
            jax.ShapeDtypeStruct((2, 1024, 256), BF16),
            jax.ShapeDtypeStruct((64, 640), BF16),
        ),
        in_specs=[hbm] * 7 + [smem] * 4,
        out_specs=(vmem, hbm, vmem),
        scratch_shapes=scratch,
        compiler_params=pltpu.CompilerParams(
            collective_id=0, has_side_effects=True, vmem_limit_bytes=60 * 2**20
        ),
        cost_estimate=pl.CostEstimate(
            flops=40_000_000_000, bytes_accessed=24 * 2**20, transcendentals=36_000_000
        ),
        name="attend_and_project",
    )(*operands)


def shards(
    prefill_queries,
    span_kv,
    prefix_cache,
    span_offsets,
    prompt_lengths,
    decode_owner,
    out_weight,
    step_queries,
    step_kv,
    decode_cache,
    contexts,
):
    prefill_out, landed, decode_out = run_kernel(
        prefill_queries,
        span_kv.reshape(2, 64, 256),
        prefix_cache.reshape(2, 2048, 256),
        out_weight,
        step_queries,
        step_kv.reshape(4, 16, 256),
        decode_cache.reshape(16, 1024, 256),
        span_offsets,
        prompt_lengths,
        decode_owner,
        contexts,
    )
    return (prefill_out, landed.reshape(2, 1024, 1, 256), decode_out.reshape(4, 16, 640))


def solution(mesh):
    placed = (
        P(None, "seq", ("head", "section")),
        P(None, "seq", ("head", "section"), None),
        P(None, "seq", ("head", "section"), None),
        P(),
        P(),
        P(),
        P(("head", "section"), None),
        P(None, "seq", ("head", "section")),
        P(None, "seq", ("head", "section"), None),
        P("seq", None, ("head", "section"), None),
        P("seq"),
    )
    return jax.shard_map(
        shards,
        mesh=mesh,
        in_specs=placed,
        out_specs=(
            P(None, "seq", ("head", "section")),
            P("seq", None, ("head", "section"), None),
            P(None, "seq", ("head", "section")),
        ),
        check_vma=False,
    )
```

```python
import functools
import math

import jax
import jax.numpy as jnp
from jax import lax
from jax.experimental import pallas as pl
from jax.experimental.pallas import tpu as pltpu
from jax.sharding import PartitionSpec as P

MESH = pl.DeviceIdType.MESH
BF16 = jnp.bfloat16
F32 = jnp.float32
HIDDEN = -1e30
FLOOR = -1e29
LOG2E = math.log2(math.e)


def mul(a, b):
    return lax.dot_general(a, b, (((1,), (0,)), ((), ())), preferred_element_type=F32)


def mul_t(a, b):
    return lax.dot_general(a, b, (((1,), (1,)), ((), ())), preferred_element_type=F32)


def kernel(
    pq, skv, pre, w, sq, stepkv, dcache, offs, lens, owner, ctx,
    out_p, out_l, out_d,
    pqv, qst, qg, kv, sk, wb, dcb, sqv, skvv, dqf, dsf, qhl, acc, mbuf, okeep, lkeep,
    zo_s, zl_s, zo_r, zl_r, xo_s, xl_s, xo_r, xl_r, att_s, att_r, decf,
    p_s, p_r, p_own, spg, lnd,
    s_q, s_kv, s_w, s_dc, s_dq,
    sibq_s, sibq_r, sibkv_s, sibkv_r, sibsk_s, sibsk_r, siba_s, siba_r,
    agz_s, agz_r, agx_s, agx_r, rzo_s, rzo_r, rzl_s, rzl_r, rxo_s, rxo_r, rxl_s, rxl_r,
    o_s, o_r, sp_s, sp_r, sps_s, sps_r, s_l,
):
    seq, head, sec = lax.axis_index("seq"), lax.axis_index("head"), lax.axis_index("section")
    x, z, k = seq // 4, (seq // 2) % 2, seq % 2
    other = 1 - k
    chip = x * 2 + z
    scale = LOG2E / math.sqrt(128)
    swapped = ((lens[1] - offs[1]) > (lens[0] - offs[0])).astype(jnp.int32)

    def prompt_of(phase):
        return jnp.where(phase == 0, swapped, 1 - swapped)

    def fill_of(prompt):
        return lens[prompt] - offs[prompt]

    def at_seq(xx, zz, kk):
        return (xx * 4 + zz * 2 + kk, head, sec)

    sibling = at_seq(x, z, other)
    zpeer = at_seq(x, 1 - z, k)

    def xpeer(d):
        return at_seq((x + d) % 4, z, k)

    def plane_peer(n):
        return at_seq((x + n // 2) % 4, (z + n) % 2, k)

    def hpeer(n):
        return (seq, (head + n // 2) % 4, (sec + n) % 2)

    def remote(src, dst, ss, rs, dev):
        return pltpu.make_async_remote_copy(
            src_ref=src, dst_ref=dst, send_sem=ss, recv_sem=rs, device_id=dev, device_id_type=MESH
        )

    barrier = pltpu.get_barrier_semaphore()
    peers = [sibling] + [plane_peer(n) for n in range(1, 8)] + [hpeer(n) for n in range(1, 8)]
    for dev in peers:
        pl.semaphore_signal(barrier, inc=1, device_id=dev, device_id_type=MESH)
    pl.semaphore_wait(barrier, len(peers))

    q_copy = pltpu.make_async_copy(pq, pqv, s_q.at[0])

    def sib_q(r):
        return remote(qst.at[r], qg.at[chip, r, k], sibq_s.at[r], sibq_r.at[r], sibling)

    def got_sib_q(r):
        return remote(qst.at[r], qg.at[chip, r, other], sibq_s.at[r], sibq_r.at[r], sibling)

    def own_kv(r):
        return pltpu.make_async_copy(pre.at[r], kv.at[r, k], s_kv.at[r])

    def own_sk(r):
        return pltpu.make_async_copy(skv.at[r], sk.at[r, k], s_kv.at[2 + r])

    def sib_kv(r, kk):
        return remote(pre.at[r], kv.at[r, kk], sibkv_s.at[r], sibkv_r.at[r], sibling)

    def sib_sk(r, kk):
        return remote(skv.at[r], sk.at[r, kk], sibsk_s.at[r], sibsk_r.at[r], sibling)

    def dec_copy(b):
        return pltpu.make_async_copy(dcache.at[b], dcb.at[b], s_dc.at[b])

    def w_copy(p):
        return pltpu.make_async_copy(w.at[:, pl.ds(p * 640, 640)], wb.at[p], s_w.at[p])

    q_copy.start()
    sq_copy = pltpu.make_async_copy(sq, sqv, s_dq.at[0])
    st_copy = pltpu.make_async_copy(stepkv, skvv, s_dq.at[1])
    sq_copy.start()
    st_copy.start()
    for b in range(4):
        dec_copy(b).start()
    q_copy.wait()
    for r in range(2):
        mine = jnp.where(prompt_of(r) == 0, pqv[0].astype(F32), pqv[1].astype(F32)).astype(BF16)
        left, right = mine[:, 0:512].astype(F32), mine[:, 512:1024].astype(F32)
        qg[chip, r, k] = jnp.where(k == 0, left, right).astype(BF16)
        qst[r] = jnp.where(k == 0, right, left).astype(BF16)
        sib_q(r).start()
    for r in range(2):
        sib_sk(r, k).start()
        sib_kv(r, k).start()
        own_sk(r).start()
        own_kv(r).start()
    for b in range(4, 16):
        dec_copy(b).start()
    for p in range(8):
        w_copy(p).start()

    def gz(j, r):
        return remote(qg.at[j, r], qg.at[j, r], agz_s.at[r], agz_r.at[r], zpeer)

    def gx(j, d, f, r):
        return remote(
            qg.at[j, r], qg.at[j, r], agx_s.at[d, f, r], agx_r.at[d, f, r], xpeer(4 - d)
        )

    def task_chip(d, f):
        return ((x + d) % 4) * 2 + (z + f) % 2

    got_sib_q(0).wait_recv()
    gz(chip, 0).start()
    gx(chip, 1, 0, 0).start()
    gx(chip, 3, 0, 0).start()
    got_sib_q(1).wait_recv()

    sq_copy.wait()
    st_copy.wait()
    for t in range(4):
        step_q = sqv[t].astype(F32)
        for h in range(8):
            dqf[:, h * 4 + t, :] = step_q[:, h * 128 : h * 128 + 128]
        dsf[:, 4 + t, :] = skvv[t].astype(F32)

    def decode_group(g, carry):
        row_step = lax.broadcasted_iota(jnp.int32, (32, 1024), 0) % 4
        key_id = lax.broadcasted_iota(jnp.int32, (32, 1024), 1)
        fresh = (key_id >= 1020) & (key_id - 1020 <= row_step)
        step_rows = lax.broadcasted_iota(jnp.int32, (8, 256), 0) >= 4
        for e in range(4):
            b = g * 4 + e
            dec_copy(b).wait()
            tail = dcb[b, pl.ds(1008, 16), :].astype(F32)
            tail = jnp.concatenate([tail[0:8], jnp.where(step_rows, dsf[b], tail[8:16])], axis=0)
            dcb[b, pl.ds(1008, 16), :] = tail.astype(BF16)
            s = mul_t(dqf[b].astype(BF16), dcb[b, :, 0:128]) * scale
            seen = fresh | (key_id < ctx[b])
            s = jnp.where(seen, s, HIDDEN)
            m = jnp.max(s, axis=1, keepdims=True)
            pw = jnp.exp2(s - m)
            den = jnp.sum(pw, axis=1, keepdims=True)
            o = mul(pw.astype(BF16), dcb[b, :, 128:256]) / den
            for h in range(8):
                decf[b, :, h * 128 : h * 128 + 128] = o[h * 4 : h * 4 + 4, :]
        return carry

    lax.fori_loop(0, 1, decode_group, 0)
    gz(task_chip(0, 1), 0).wait_recv()
    gx(task_chip(0, 1), 1, 1, 0).start()
    gx(task_chip(0, 1), 3, 1, 0).start()
    gx(chip, 2, 0, 0).start()
    gx(task_chip(0, 1), 2, 1, 0).start()
    lax.fori_loop(1, 3, decode_group, 0)
    gz(chip, 1).start()
    lax.fori_loop(3, 4, decode_group, 0)

    def rz_o(t):
        return remote(zo_s.at[t], zo_r.at[t], rzo_s.at[t], rzo_r.at[t], zpeer)

    def rz_l(t):
        return remote(zl_s.at[t], zl_r.at[t], rzl_s.at[t], rzl_r.at[t], zpeer)

    def rx_o(r, d):
        return remote(xo_s.at[r, d], xo_r.at[r, d], rxo_s.at[r, d], rxo_r.at[r, d], xpeer(d))

    def rx_l(r, d):
        return remote(xl_s.at[r, d], xl_r.at[r, d], rxl_s.at[r, d], rxl_r.at[r, d], xpeer(d))

    def spread(row):
        return jnp.transpose(jnp.broadcast_to(row, (128, 512)))

    def pack(col):
        return jnp.transpose(col)[0:8, :]

    def task_step(t):
        return (t + t // 4) % 4

    def chain(t):
        r, d = t // 4, task_step(t)
        rz_o(t).wait_recv()
        rz_l(t).wait_recv()
        l0, l1 = lkeep[...], spread(zl_r[t, 0:1, :])
        top = jnp.maximum(l0, l1)
        e0, e1 = jnp.exp2(l0 - top), jnp.exp2(l1 - top)
        den = e0 + e1
        o = ((okeep[...] * e0 + zo_r[t].astype(F32) * e1) / den).astype(BF16)
        lse = pack(top + jnp.log(den) * LOG2E)

        @pl.when(d == 0)
        def _():
            xo_r[r, 0] = o
            xl_r[r, 0] = lse

        @pl.when(d != 0)
        def _():
            xo_s[r, d] = o
            xl_s[r, d] = lse
            rx_o(r, d).start()
            rx_l(r, d).start()

    def sib_att(r):
        return remote(att_s.at[r, other], att_r.at[r, k], siba_s.at[r], siba_r.at[r], sibling)

    def got_sib_att(r):
        return remote(att_s.at[r, other], att_r.at[r, other], siba_s.at[r], siba_r.at[r], sibling)

    def settle(r):
        for d in (1, 2, 3):
            rx_o(r, d).wait_recv()
            rx_l(r, d).wait_recv()
        ls = [spread(xl_r[r, d, 0:1, :]) for d in range(4)]
        top = functools.reduce(jnp.maximum, ls)
        es = [jnp.exp2(v - top) for v in ls]
        den = functools.reduce(jnp.add, es)
        num = functools.reduce(jnp.add, [es[d] * xo_r[r, d].astype(F32) for d in range(4)])
        token = lax.broadcasted_iota(jnp.int32, (512, 128), 0) % 128 + chip * 128
        o = jnp.where(token < fill_of(prompt_of(r)), num / den, 0.0).astype(BF16)
        for h in range(4):
            for kk in range(2):
                att_s[r, kk, :, h * 128 : h * 128 + 128] = o[h * 128 + kk * 64 : h * 128 + kk * 64 + 64]
        sib_att(r).start()
        att_r[r, k] = att_s[r, k]

    def to_owner(stage, n):
        return remote(
            p_s.at[stage, n], p_r.at[stage, n], o_s.at[stage, n], o_r.at[stage, n], hpeer(n)
        )

    def column_block(n):
        return ((head + n // 2) % 4) * 2 + (sec + n) % 2

    def project(lhs, n):
        p = column_block(n)
        return mul(lhs[0], wb[p, 0:512, :]) + mul(lhs[1], wb[p, 512:1024, :])

    def project_stage(stage, lhs):
        def step(i, carry):
            n = (i * 5) % 8
            p_s[stage, n] = project(lhs, n).astype(BF16)
            to_owner(stage, n).start()
            return carry

        lax.fori_loop(1, 8, step, 0)
        p_own[stage] = project(lhs, 0)

    def project_prompt(r):
        got_sib_att(r).wait_recv()
        project_stage(1 + r, [att_r[r, h] for h in range(2)])

    def span_out(n):
        return remote(sk.at[k], spg.at[k, chip], sp_s.at[n], sp_r.at[n], plane_peer(n))

    def span_in(n):
        source = ((x - n // 2) % 4) * 2 + (z + n) % 2
        return remote(sk.at[k], spg.at[k, source], sp_s.at[n], sp_r.at[n], plane_peer(n))

    def span_swap(r):
        return remote(spg.at[r], spg.at[r], sps_s.at[0], sps_r.at[0], sibling)

    def land_copy():
        return pltpu.make_async_copy(lnd, out_l, s_l.at[0])

    def land():
        span_swap(other).wait_recv()
        for r in range(2):
            token = lax.broadcasted_iota(jnp.int32, (1024, 256), 0)
            limit = jnp.where(owner[r] == seq, fill_of(r), 0)
            rows = spg[r].reshape(1024, 256).astype(F32)
            lnd[r] = jnp.where(token < limit, rows, 0.0).astype(BF16)
        land_copy().start()

    for p in range(8):
        w_copy(p).wait()
    dec = jnp.concatenate([decf[:, t, :] for t in range(4)], axis=0).astype(BF16)
    project_stage(0, [dec[:, h * 512 : h * 512 + 512] for h in range(2)])

    for r in range(2):
        own_kv(r).wait()
        own_sk(r).wait()
        sib_kv(r, other).wait_recv()
        sib_sk(r, other).wait_recv()

    ones = jnp.ones((256, 128), BF16)

    def load_queries(r, d):
        for f in range(2):
            src = qg[task_chip(d, f), r].reshape(128, 512).astype(F32) * scale
            base = 512 * (1 - f)
            for h in range(4):
                part = src[:, h * 128 : h * 128 + 128]
                hi = part.astype(BF16)
                qhl[base + h * 128 : base + h * 128 + 128, 0:128] = hi
                qhl[base + h * 128 : base + h * 128 + 128, 128:256] = (part - hi.astype(F32)).astype(BF16)

    def attend(prompt, d, lo, n):
        limit, seen_prefix = fill_of(prompt), offs[prompt]
        q = qhl[lo : lo + n, :]
        rows = sk[prompt].reshape(128, 256)
        s = mul_t(q, jnp.concatenate([rows[:, 0:128], rows[:, 0:128]], axis=1))
        row = lax.broadcasted_iota(jnp.int32, (n, 128), 0) + lo
        key = lax.broadcasted_iota(jnp.int32, (n, 128), 1) + chip * 128
        token = row % 128 + 128 * jnp.where(row < 512, task_chip(d, 1), task_chip(d, 0))
        seen = (key <= token) & (key < limit)
        s = jnp.where(seen, s, HIDDEN)
        m = jnp.maximum(jnp.broadcast_to(jnp.max(s, axis=1, keepdims=True), (n, 128)), FLOOR)
        total = mul(
            jnp.exp2(s - m).astype(BF16), jnp.concatenate([rows[:, 128:256], ones[0:128]], axis=1)
        )
        for e in range(16):
            src, n0 = e // 8, e % 8 * 256
            kb = kv[prompt, src, n0 : n0 + 256, 0:128]
            vb = kv[prompt, src, n0 : n0 + 256, 128:256]
            pos = lax.broadcasted_iota(jnp.int32, (1, 256), 1) + (chip * 4096 + src * 2048 + n0)
            bias = jnp.where(pos < seen_prefix, 0.0, HIDDEN)
            s = mul_t(q, jnp.concatenate([kb, kb], axis=1)) + bias
            mn = jnp.maximum(m, jnp.broadcast_to(jnp.max(s, axis=1, keepdims=True), (n, 128)))
            pw = jnp.exp2(s - jnp.concatenate([mn, mn], axis=1)).astype(BF16)
            rescale = jnp.exp2(m - mn)
            total = total * jnp.concatenate([rescale, rescale], axis=1) + mul(
                pw, jnp.concatenate([vb, ones], axis=1)
            )
            m = mn
        den = jnp.maximum(total[:, 128:256], 1e-30)
        acc[lo : lo + n, :] = total[:, 0:128] / den
        mbuf[lo : lo + n, :] = m + jnp.log(den) * LOG2E

    def send_z(t):
        zo_s[t] = acc[0:512].astype(BF16)
        zl_s[t] = pack(mbuf[0:512])
        rz_o(t).start()
        rz_l(t).start()

    def keep():
        okeep[...] = acc[512:1024]
        lkeep[...] = mbuf[512:1024]

    def await_queries(r, d):
        for f in range(2):
            gx(task_chip(d, f), d, f, r).wait_recv()

    def task(t, carry):
        r, d = t // 4, task_step(t)

        @pl.when(d != 0)
        def _():
            await_queries(r, d)

        load_queries(r, d)
        attend(prompt_of(r), d, 0, 1024)

        @pl.when(t > 0)
        def _():
            chain(t - 1)

        send_z(t)
        keep()

        @pl.when(t == 0)
        def _():
            gz(task_chip(0, 1), 1).wait_recv()
            for d2 in (1, 3, 2):
                gx(chip, d2, 0, 1).start()
                gx(task_chip(0, 1), d2, 1, 1).start()

        @pl.when(t == 2)
        def _():
            spg[k, chip] = sk[k]
            for n in range(1, 8):
                span_out(n).start()

        @pl.when(t == 4)
        def _():
            for n in range(1, 8):
                span_in(n).wait_recv()
            span_swap(k).start()

        @pl.when(t == 5)
        def _():
            settle(0)
            land()

        @pl.when(t == 6)
        def _():
            project_prompt(0)

        return carry

    lax.fori_loop(0, 7, task, 0)
    load_queries(1, 0)
    attend(prompt_of(1), 0, 0, 512)
    send_z(7)
    chain(6)
    attend(prompt_of(1), 0, 512, 512)
    keep()
    chain(7)
    settle(1)
    project_prompt(1)

    def gathered(stage):
        total = p_own[stage]
        for n in range(1, 8):
            to_owner(stage, n).wait_recv()
            total = total + p_r[stage, n].astype(F32)
        return total.astype(BF16)

    out_d[...] = gathered(0)
    first = gathered(1)
    second = gathered(2)
    straight = swapped == 0
    out_p[0] = jnp.where(straight, first.astype(F32), second.astype(F32)).astype(BF16)
    out_p[1] = jnp.where(straight, second.astype(F32), first.astype(F32)).astype(BF16)

    for r in range(2):
        gz(chip, r).wait_send()
        for d in (1, 2, 3):
            gx(chip, d, 0, r).wait_send()
            gx(task_chip(0, 1), d, 1, r).wait_send()
        sib_q(r).wait_send()
        sib_kv(r, k).wait_send()
        sib_sk(r, k).wait_send()
        sib_att(r).wait_send()
        for d in (1, 2, 3):
            rx_o(r, d).wait_send()
            rx_l(r, d).wait_send()
    for t in range(8):
        rz_o(t).wait_send()
        rz_l(t).wait_send()
    span_swap(k).wait_send()
    land_copy().wait()
    for n in range(1, 8):
        span_out(n).wait_send()
        for stage in range(3):
            to_owner(stage, n).wait_send()


def hand_over_kernel(a, b, c, out_a, out_b, out_c):
    out_a[...] = a[...]
    out_b[...] = b[...]
    out_c[...] = c[...]


def hand_over(*results):
    vmem = pl.BlockSpec(memory_space=pltpu.VMEM)
    return pl.pallas_call(
        hand_over_kernel,
        out_shape=tuple(jax.ShapeDtypeStruct(r.shape, r.dtype) for r in results),
        in_specs=[vmem] * 3,
        out_specs=(vmem,) * 3,
        name="hand_over",
    )(*results)


def run_kernel(*operands):
    dma = pltpu.SemaphoreType.DMA
    scratch = [
        pltpu.VMEM((2, 64, 1024), BF16),
        pltpu.VMEM((2, 64, 512), BF16),
        pltpu.VMEM((8, 2, 2, 64, 512), BF16),
        pltpu.VMEM((2, 2, 2048, 256), BF16),
        pltpu.VMEM((2, 2, 64, 256), BF16),
        pltpu.VMEM((8, 1024, 640), BF16),
        pltpu.VMEM((16, 1024, 256), BF16),
        pltpu.VMEM((4, 16, 1024), BF16),
        pltpu.VMEM((4, 16, 256), BF16),
        pltpu.VMEM((16, 32, 128), F32),
        pltpu.VMEM((16, 8, 256), F32),
        pltpu.VMEM((1024, 256), BF16),
        pltpu.VMEM((1024, 128), F32),
        pltpu.VMEM((1024, 128), F32),
        pltpu.VMEM((512, 128), F32),
        pltpu.VMEM((512, 128), F32),
        pltpu.VMEM((8, 512, 128), BF16),
        pltpu.VMEM((8, 8, 512), F32),
        pltpu.VMEM((8, 512, 128), BF16),
        pltpu.VMEM((8, 8, 512), F32),
        pltpu.VMEM((2, 4, 512, 128), BF16),
        pltpu.VMEM((2, 4, 8, 512), F32),
        pltpu.VMEM((2, 4, 512, 128), BF16),
        pltpu.VMEM((2, 4, 8, 512), F32),
        pltpu.VMEM((2, 2, 64, 512), BF16),
        pltpu.VMEM((2, 2, 64, 512), BF16),
        pltpu.VMEM((16, 4, 1024), F32),
        pltpu.VMEM((3, 8, 64, 640), BF16),
        pltpu.VMEM((3, 8, 64, 640), BF16),
        pltpu.VMEM((3, 64, 640), F32),
        pltpu.VMEM((2, 8, 2, 64, 256), BF16),
        pltpu.VMEM((2, 1024, 256), BF16),
        dma((1,)), dma((4,)), dma((8,)), dma((16,)), dma((2,)),
        dma((2,)), dma((2,)), dma((2,)), dma((2,)), dma((2,)), dma((2,)), dma((2,)), dma((2,)),
        dma((2,)), dma((2,)), dma((4, 2, 2)), dma((4, 2, 2)),
        dma((8,)), dma((8,)), dma((8,)), dma((8,)),
        dma((2, 4)), dma((2, 4)), dma((2, 4)), dma((2, 4)),
        dma((3, 8)), dma((3, 8)), dma((8,)), dma((8,)), dma((1,)), dma((1,)), dma((1,)),
    ]
    hbm = pl.BlockSpec(memory_space=pl.ANY)
    smem = pl.BlockSpec(memory_space=pltpu.SMEM)
    vmem = pl.BlockSpec(memory_space=pltpu.VMEM)
    return pl.pallas_call(
        kernel,
        out_shape=(
            jax.ShapeDtypeStruct((2, 64, 640), BF16),
            jax.ShapeDtypeStruct((2, 1024, 256), BF16),
            jax.ShapeDtypeStruct((64, 640), BF16),
        ),
        in_specs=[hbm] * 7 + [smem] * 4,
        out_specs=(vmem, hbm, vmem),
        scratch_shapes=scratch,
        compiler_params=pltpu.CompilerParams(
            collective_id=0, has_side_effects=True, vmem_limit_bytes=60 * 2**20
        ),
        cost_estimate=pl.CostEstimate(
            flops=40_000_000_000, bytes_accessed=24 * 2**20, transcendentals=36_000_000
        ),
        name="attend_and_project",
    )(*operands)


def shards(
    prefill_queries,
    span_kv,
    prefix_cache,
    span_offsets,
    prompt_lengths,
    decode_owner,
    out_weight,
    step_queries,
    step_kv,
    decode_cache,
    contexts,
):
    prefill_out, landed, decode_out = run_kernel(
        prefill_queries,
        span_kv.reshape(2, 64, 256),
        prefix_cache.reshape(2, 2048, 256),
        out_weight,
        step_queries,
        step_kv.reshape(4, 16, 256),
        decode_cache.reshape(16, 1024, 256),
        span_offsets,
        prompt_lengths,
        decode_owner,
        contexts,
    )
    prefill_out, landed, decode_out = hand_over(prefill_out, landed, decode_out)
    return (prefill_out, landed.reshape(2, 1024, 1, 256), decode_out.reshape(4, 16, 640))


def solution(mesh):
    placed = (
        P(None, "seq", ("head", "section")),
        P(None, "seq", ("head", "section"), None),
        P(None, "seq", ("head", "section"), None),
        P(),
        P(),
        P(),
        P(("head", "section"), None),
        P(None, "seq", ("head", "section")),
        P(None, "seq", ("head", "section"), None),
        P("seq", None, ("head", "section"), None),
        P("seq"),
    )
    return jax.shard_map(
        shards,
        mesh=mesh,
        in_specs=placed,
        out_specs=(
            P(None, "seq", ("head", "section")),
            P("seq", None, ("head", "section"), None),
            P(None, "seq", ("head", "section")),
        ),
        check_vma=False,
    )
```

```python
import functools
import math

import jax
import jax.numpy as jnp
from jax import lax
from jax.experimental import pallas as pl
from jax.experimental.pallas import tpu as pltpu
from jax.sharding import PartitionSpec as P

MESH = pl.DeviceIdType.MESH
BF16 = jnp.bfloat16
F32 = jnp.float32
HIDDEN = -1e30
FLOOR = -1e29
LOG2E = math.log2(math.e)


def mul(a, b):
    return lax.dot_general(a, b, (((1,), (0,)), ((), ())), preferred_element_type=F32)


def mul_t(a, b):
    return lax.dot_general(a, b, (((1,), (1,)), ((), ())), preferred_element_type=F32)


def kernel(
    pq, skv, pre, w, sq, stepkv, dcache, offs, lens, owner, ctx,
    out_p, out_l, out_d,
    pqv, qst, qg, kv, sk, wb, dcb, sqv, skvv, dqf, dsf, qhl, acc, mbuf, okeep, lkeep,
    zo_s, zl_s, zo_r, zl_r, xo_s, xl_s, xo_r, xl_r, att_s, att_r, decf,
    p_s, p_r, p_own, spg, lnd,
    s_q, s_kv, s_w, s_dc, s_dq,
    sibq_s, sibq_r, sibkv_s, sibkv_r, sibsk_s, sibsk_r, siba_s, siba_r,
    agz_s, agz_r, agx_s, agx_r, rzo_s, rzo_r, rzl_s, rzl_r, rxo_s, rxo_r, rxl_s, rxl_r,
    o_s, o_r, sp_s, sp_r, sps_s, sps_r, s_l,
):
    seq, head, sec = lax.axis_index("seq"), lax.axis_index("head"), lax.axis_index("section")
    x, z, k = seq // 4, (seq // 2) % 2, seq % 2
    other = 1 - k
    chip = x * 2 + z
    scale = LOG2E / math.sqrt(128)
    swapped = ((lens[1] - offs[1]) > (lens[0] - offs[0])).astype(jnp.int32)

    def prompt_of(phase):
        return jnp.where(phase == 0, swapped, 1 - swapped)

    def fill_of(prompt):
        return lens[prompt] - offs[prompt]

    def at_seq(xx, zz, kk):
        return (xx * 4 + zz * 2 + kk, head, sec)

    sibling = at_seq(x, z, other)
    zpeer = at_seq(x, 1 - z, k)

    def xpeer(d):
        return at_seq((x + d) % 4, z, k)

    def plane_peer(n):
        return at_seq((x + n // 2) % 4, (z + n) % 2, k)

    def hpeer(n):
        return (seq, (head + n // 2) % 4, (sec + n) % 2)

    def remote(src, dst, ss, rs, dev):
        return pltpu.make_async_remote_copy(
            src_ref=src, dst_ref=dst, send_sem=ss, recv_sem=rs, device_id=dev, device_id_type=MESH
        )

    barrier = pltpu.get_barrier_semaphore()
    peers = [sibling] + [plane_peer(n) for n in range(1, 8)] + [hpeer(n) for n in range(1, 8)]
    for dev in peers:
        pl.semaphore_signal(barrier, inc=1, device_id=dev, device_id_type=MESH)

    q_copy = pltpu.make_async_copy(pq, pqv, s_q.at[0])

    def sib_q(r):
        return remote(qst.at[r], qg.at[chip, r, k], sibq_s.at[r], sibq_r.at[r], sibling)

    def got_sib_q(r):
        return remote(qst.at[r], qg.at[chip, r, other], sibq_s.at[r], sibq_r.at[r], sibling)

    def own_kv(r):
        return pltpu.make_async_copy(pre.at[r], kv.at[r, k], s_kv.at[r])

    def own_sk(r):
        return pltpu.make_async_copy(skv.at[r], sk.at[r, k], s_kv.at[2 + r])

    def sib_kv(r, kk):
        return remote(pre.at[r], kv.at[r, kk], sibkv_s.at[r], sibkv_r.at[r], sibling)

    def sib_sk(r, kk):
        return remote(skv.at[r], sk.at[r, kk], sibsk_s.at[r], sibsk_r.at[r], sibling)

    def dec_copy(b):
        return pltpu.make_async_copy(dcache.at[b], dcb.at[b], s_dc.at[b])

    def w_copy(p):
        return pltpu.make_async_copy(w.at[:, pl.ds(p * 640, 640)], wb.at[p], s_w.at[p])

    q_copy.start()
    sq_copy = pltpu.make_async_copy(sq, sqv, s_dq.at[0])
    st_copy = pltpu.make_async_copy(stepkv, skvv, s_dq.at[1])
    sq_copy.start()
    st_copy.start()
    for b in range(16):
        dec_copy(b).start()
    q_copy.wait()
    for r in range(2):
        mine = jnp.where(prompt_of(r) == 0, pqv[0].astype(F32), pqv[1].astype(F32)).astype(BF16)
        left, right = mine[:, 0:512].astype(F32), mine[:, 512:1024].astype(F32)
        qg[chip, r, k] = jnp.where(k == 0, left, right).astype(BF16)
        qst[r] = jnp.where(k == 0, right, left).astype(BF16)
    pl.semaphore_wait(barrier, len(peers))
    for r in range(2):
        sib_q(r).start()
    for r in range(2):
        sib_sk(r, k).start()
        sib_kv(r, k).start()
        own_sk(r).start()
        own_kv(r).start()
    for p in range(8):
        w_copy(p).start()

    def gz(j, r):
        return remote(qg.at[j, r], qg.at[j, r], agz_s.at[r], agz_r.at[r], zpeer)

    def gx(j, d, f, r):
        return remote(
            qg.at[j, r], qg.at[j, r], agx_s.at[d, f, r], agx_r.at[d, f, r], xpeer(4 - d)
        )

    def task_chip(d, f):
        return ((x + d) % 4) * 2 + (z + f) % 2

    got_sib_q(0).wait_recv()
    gz(chip, 0).start()
    gx(chip, 1, 0, 0).start()
    gx(chip, 3, 0, 0).start()
    got_sib_q(1).wait_recv()

    sq_copy.wait()
    st_copy.wait()
    for t in range(4):
        step_q = sqv[t].astype(F32)
        for h in range(8):
            dqf[:, h * 4 + t, :] = step_q[:, h * 128 : h * 128 + 128]
        dsf[:, 4 + t, :] = skvv[t].astype(F32)

    def decode_group(g, carry):
        row_step = lax.broadcasted_iota(jnp.int32, (32, 1024), 0) % 4
        key_id = lax.broadcasted_iota(jnp.int32, (32, 1024), 1)
        fresh = (key_id >= 1020) & (key_id - 1020 <= row_step)
        step_rows = lax.broadcasted_iota(jnp.int32, (8, 256), 0) >= 4
        for e in range(4):
            b = g * 4 + e
            dec_copy(b).wait()
            tail = dcb[b, pl.ds(1008, 16), :].astype(F32)
            tail = jnp.concatenate([tail[0:8], jnp.where(step_rows, dsf[b], tail[8:16])], axis=0)
            dcb[b, pl.ds(1008, 16), :] = tail.astype(BF16)
            s = mul_t(dqf[b].astype(BF16), dcb[b, :, 0:128]) * scale
            seen = fresh | (key_id < ctx[b])
            s = jnp.where(seen, s, HIDDEN)
            m = jnp.max(s, axis=1, keepdims=True)
            pw = jnp.exp2(s - m)
            den = jnp.sum(pw, axis=1, keepdims=True)
            o = mul(pw.astype(BF16), dcb[b, :, 128:256]) / den
            for h in range(8):
                decf[b, :, h * 128 : h * 128 + 128] = o[h * 4 : h * 4 + 4, :]
        return carry

    lax.fori_loop(0, 1, decode_group, 0)
    gz(task_chip(0, 1), 0).wait_recv()
    gx(task_chip(0, 1), 1, 1, 0).start()
    gx(task_chip(0, 1), 3, 1, 0).start()
    gx(chip, 2, 0, 0).start()
    gx(task_chip(0, 1), 2, 1, 0).start()
    lax.fori_loop(1, 3, decode_group, 0)
    gz(chip, 1).start()
    lax.fori_loop(3, 4, decode_group, 0)

    def rz_o(t):
        return remote(zo_s.at[t], zo_r.at[t], rzo_s.at[t], rzo_r.at[t], zpeer)

    def rz_l(t):
        return remote(zl_s.at[t], zl_r.at[t], rzl_s.at[t], rzl_r.at[t], zpeer)

    def rx_o(r, d):
        return remote(xo_s.at[r, d], xo_r.at[r, d], rxo_s.at[r, d], rxo_r.at[r, d], xpeer(d))

    def rx_l(r, d):
        return remote(xl_s.at[r, d], xl_r.at[r, d], rxl_s.at[r, d], rxl_r.at[r, d], xpeer(d))

    def spread(row):
        return jnp.transpose(jnp.broadcast_to(row, (128, 512)))

    def pack(col):
        return jnp.transpose(col)[0:8, :]

    def task_step(t):
        return (t + t // 4) % 4

    def chain(t):
        r, d = t // 4, task_step(t)
        rz_o(t).wait_recv()
        rz_l(t).wait_recv()
        l0, l1 = lkeep[...], spread(zl_r[t, 0:1, :])
        top = jnp.maximum(l0, l1)
        e0, e1 = jnp.exp2(l0 - top), jnp.exp2(l1 - top)
        den = e0 + e1
        o = ((okeep[...] * e0 + zo_r[t].astype(F32) * e1) / den).astype(BF16)
        lse = pack(top + jnp.log(den) * LOG2E)

        @pl.when(d == 0)
        def _():
            xo_r[r, 0] = o
            xl_r[r, 0] = lse

        @pl.when(d != 0)
        def _():
            xo_s[r, d] = o
            xl_s[r, d] = lse
            rx_o(r, d).start()
            rx_l(r, d).start()

    def sib_att(r):
        return remote(att_s.at[r, other], att_r.at[r, k], siba_s.at[r], siba_r.at[r], sibling)

    def got_sib_att(r):
        return remote(att_s.at[r, other], att_r.at[r, other], siba_s.at[r], siba_r.at[r], sibling)

    def settle(r):
        for d in (1, 2, 3):
            rx_o(r, d).wait_recv()
            rx_l(r, d).wait_recv()
        ls = [spread(xl_r[r, d, 0:1, :]) for d in range(4)]
        top = functools.reduce(jnp.maximum, ls)
        es = [jnp.exp2(v - top) for v in ls]
        den = functools.reduce(jnp.add, es)
        num = functools.reduce(jnp.add, [es[d] * xo_r[r, d].astype(F32) for d in range(4)])
        token = lax.broadcasted_iota(jnp.int32, (512, 128), 0) % 128 + chip * 128
        o = jnp.where(token < fill_of(prompt_of(r)), num / den, 0.0).astype(BF16)
        for h in range(4):
            for kk in range(2):
                att_s[r, kk, :, h * 128 : h * 128 + 128] = o[h * 128 + kk * 64 : h * 128 + kk * 64 + 64]
        sib_att(r).start()
        att_r[r, k] = att_s[r, k]

    def to_owner(stage, n):
        return remote(
            p_s.at[stage, n], p_r.at[stage, n], o_s.at[stage, n], o_r.at[stage, n], hpeer(n)
        )

    def column_block(n):
        return ((head + n // 2) % 4) * 2 + (sec + n) % 2

    def project(lhs, n):
        p = column_block(n)
        return mul(lhs[0], wb[p, 0:512, :]) + mul(lhs[1], wb[p, 512:1024, :])

    def project_stage(stage, lhs):
        def step(i, carry):
            n = (i * 5) % 8
            p_s[stage, n] = project(lhs, n).astype(BF16)
            to_owner(stage, n).start()
            return carry

        lax.fori_loop(1, 8, step, 0)
        p_own[stage] = project(lhs, 0)

    def project_prompt(r):
        got_sib_att(r).wait_recv()
        project_stage(1 + r, [att_r[r, h] for h in range(2)])

    def span_out(n):
        return remote(sk.at[k], spg.at[k, chip], sp_s.at[n], sp_r.at[n], plane_peer(n))

    def span_in(n):
        source = ((x - n // 2) % 4) * 2 + (z + n) % 2
        return remote(sk.at[k], spg.at[k, source], sp_s.at[n], sp_r.at[n], plane_peer(n))

    def span_swap(r):
        return remote(spg.at[r], spg.at[r], sps_s.at[0], sps_r.at[0], sibling)

    def land_copy():
        return pltpu.make_async_copy(lnd, out_l, s_l.at[0])

    def land():
        span_swap(other).wait_recv()
        for r in range(2):
            token = lax.broadcasted_iota(jnp.int32, (1024, 256), 0)
            limit = jnp.where(owner[r] == seq, fill_of(r), 0)
            rows = spg[r].reshape(1024, 256).astype(F32)
            lnd[r] = jnp.where(token < limit, rows, 0.0).astype(BF16)
        land_copy().start()

    for p in range(8):
        w_copy(p).wait()
    dec = jnp.concatenate([decf[:, t, :] for t in range(4)], axis=0).astype(BF16)
    project_stage(0, [dec[:, h * 512 : h * 512 + 512] for h in range(2)])

    for r in range(2):
        own_kv(r).wait()
        own_sk(r).wait()
        sib_kv(r, other).wait_recv()
        sib_sk(r, other).wait_recv()

    ones = jnp.ones((256, 128), BF16)

    def load_queries(r, d):
        for f in range(2):
            src = qg[task_chip(d, f), r].reshape(128, 512).astype(F32) * scale
            base = 512 * (1 - f)
            for h in range(4):
                part = src[:, h * 128 : h * 128 + 128]
                hi = part.astype(BF16)
                qhl[base + h * 128 : base + h * 128 + 128, 0:128] = hi
                qhl[base + h * 128 : base + h * 128 + 128, 128:256] = (part - hi.astype(F32)).astype(BF16)

    def attend(prompt, d, lo, n):
        limit, seen_prefix = fill_of(prompt), offs[prompt]
        q = qhl[lo : lo + n, :]
        rows = sk[prompt].reshape(128, 256)
        s = mul_t(q, jnp.concatenate([rows[:, 0:128], rows[:, 0:128]], axis=1))
        row = lax.broadcasted_iota(jnp.int32, (n, 128), 0) + lo
        key = lax.broadcasted_iota(jnp.int32, (n, 128), 1) + chip * 128
        token = row % 128 + 128 * jnp.where(row < 512, task_chip(d, 1), task_chip(d, 0))
        seen = (key <= token) & (key < limit)
        s = jnp.where(seen, s, HIDDEN)
        m = jnp.maximum(jnp.broadcast_to(jnp.max(s, axis=1, keepdims=True), (n, 128)), FLOOR)
        total = mul(
            jnp.exp2(s - m).astype(BF16), jnp.concatenate([rows[:, 128:256], ones[0:128]], axis=1)
        )
        for e in range(16):
            src, n0 = e // 8, e % 8 * 256
            kb = kv[prompt, src, n0 : n0 + 256, 0:128]
            vb = kv[prompt, src, n0 : n0 + 256, 128:256]
            pos = lax.broadcasted_iota(jnp.int32, (1, 256), 1) + (chip * 4096 + src * 2048 + n0)
            bias = jnp.where(pos < seen_prefix, 0.0, HIDDEN)
            s = mul_t(q, jnp.concatenate([kb, kb], axis=1)) + bias
            mn = jnp.maximum(m, jnp.broadcast_to(jnp.max(s, axis=1, keepdims=True), (n, 128)))
            pw = jnp.exp2(s - jnp.concatenate([mn, mn], axis=1)).astype(BF16)
            rescale = jnp.exp2(m - mn)
            total = total * jnp.concatenate([rescale, rescale], axis=1) + mul(
                pw, jnp.concatenate([vb, ones], axis=1)
            )
            m = mn
        den = jnp.maximum(total[:, 128:256], 1e-30)
        acc[lo : lo + n, :] = total[:, 0:128] / den
        mbuf[lo : lo + n, :] = m + jnp.log(den) * LOG2E

    def send_z(t):
        zo_s[t] = acc[0:512].astype(BF16)
        zl_s[t] = pack(mbuf[0:512])
        rz_o(t).start()
        rz_l(t).start()

    def keep():
        okeep[...] = acc[512:1024]
        lkeep[...] = mbuf[512:1024]

    def await_queries(r, d):
        for f in range(2):
            gx(task_chip(d, f), d, f, r).wait_recv()

    def task(t, carry):
        r, d = t // 4, task_step(t)

        @pl.when(d != 0)
        def _():
            await_queries(r, d)

        load_queries(r, d)
        attend(prompt_of(r), d, 0, 1024)

        @pl.when(t > 0)
        def _():
            chain(t - 1)

        send_z(t)
        keep()

        @pl.when(t == 0)
        def _():
            gz(task_chip(0, 1), 1).wait_recv()
            for d2 in (1, 3, 2):
                gx(chip, d2, 0, 1).start()
                gx(task_chip(0, 1), d2, 1, 1).start()

        @pl.when(t == 2)
        def _():
            spg[k, chip] = sk[k]
            for n in range(1, 8):
                span_out(n).start()

        @pl.when(t == 4)
        def _():
            for n in range(1, 8):
                span_in(n).wait_recv()
            span_swap(k).start()

        @pl.when(t == 5)
        def _():
            settle(0)
            land()

        @pl.when(t == 6)
        def _():
            project_prompt(0)

        return carry

    lax.fori_loop(0, 7, task, 0)
    load_queries(1, 0)
    attend(prompt_of(1), 0, 0, 512)
    send_z(7)
    chain(6)
    attend(prompt_of(1), 0, 512, 512)
    keep()
    chain(7)
    settle(1)
    project_prompt(1)

    def gathered(stage):
        total = p_own[stage]
        for n in range(1, 8):
            to_owner(stage, n).wait_recv()
            total = total + p_r[stage, n].astype(F32)
        return total.astype(BF16)

    out_d[...] = gathered(0)
    first = gathered(1)
    second = gathered(2)
    straight = swapped == 0
    out_p[0] = jnp.where(straight, first.astype(F32), second.astype(F32)).astype(BF16)
    out_p[1] = jnp.where(straight, second.astype(F32), first.astype(F32)).astype(BF16)

    for r in range(2):
        gz(chip, r).wait_send()
        for d in (1, 2, 3):
            gx(chip, d, 0, r).wait_send()
            gx(task_chip(0, 1), d, 1, r).wait_send()
        sib_q(r).wait_send()
        sib_kv(r, k).wait_send()
        sib_sk(r, k).wait_send()
        sib_att(r).wait_send()
        for d in (1, 2, 3):
            rx_o(r, d).wait_send()
            rx_l(r, d).wait_send()
    for t in range(8):
        rz_o(t).wait_send()
        rz_l(t).wait_send()
    span_swap(k).wait_send()
    land_copy().wait()
    for n in range(1, 8):
        span_out(n).wait_send()
        for stage in range(3):
            to_owner(stage, n).wait_send()


def hand_over_kernel(a, b, c, out_a, out_b, out_c):
    out_a[...] = a[...]
    out_b[...] = b[...]
    out_c[...] = c[...]


def hand_over(*results):
    vmem = pl.BlockSpec(memory_space=pltpu.VMEM)
    return pl.pallas_call(
        hand_over_kernel,
        out_shape=tuple(jax.ShapeDtypeStruct(r.shape, r.dtype) for r in results),
        in_specs=[vmem] * 3,
        out_specs=(vmem,) * 3,
        name="hand_over",
    )(*results)


def run_kernel(*operands):
    dma = pltpu.SemaphoreType.DMA
    scratch = [
        pltpu.VMEM((2, 64, 1024), BF16),
        pltpu.VMEM((2, 64, 512), BF16),
        pltpu.VMEM((8, 2, 2, 64, 512), BF16),
        pltpu.VMEM((2, 2, 2048, 256), BF16),
        pltpu.VMEM((2, 2, 64, 256), BF16),
        pltpu.VMEM((8, 1024, 640), BF16),
        pltpu.VMEM((16, 1024, 256), BF16),
        pltpu.VMEM((4, 16, 1024), BF16),
        pltpu.VMEM((4, 16, 256), BF16),
        pltpu.VMEM((16, 32, 128), F32),
        pltpu.VMEM((16, 8, 256), F32),
        pltpu.VMEM((1024, 256), BF16),
        pltpu.VMEM((1024, 128), F32),
        pltpu.VMEM((1024, 128), F32),
        pltpu.VMEM((512, 128), F32),
        pltpu.VMEM((512, 128), F32),
        pltpu.VMEM((8, 512, 128), BF16),
        pltpu.VMEM((8, 8, 512), F32),
        pltpu.VMEM((8, 512, 128), BF16),
        pltpu.VMEM((8, 8, 512), F32),
        pltpu.VMEM((2, 4, 512, 128), BF16),
        pltpu.VMEM((2, 4, 8, 512), F32),
        pltpu.VMEM((2, 4, 512, 128), BF16),
        pltpu.VMEM((2, 4, 8, 512), F32),
        pltpu.VMEM((2, 2, 64, 512), BF16),
        pltpu.VMEM((2, 2, 64, 512), BF16),
        pltpu.VMEM((16, 4, 1024), F32),
        pltpu.VMEM((3, 8, 64, 640), BF16),
        pltpu.VMEM((3, 8, 64, 640), BF16),
        pltpu.VMEM((3, 64, 640), F32),
        pltpu.VMEM((2, 8, 2, 64, 256), BF16),
        pltpu.VMEM((2, 1024, 256), BF16),
        dma((1,)), dma((4,)), dma((8,)), dma((16,)), dma((2,)),
        dma((2,)), dma((2,)), dma((2,)), dma((2,)), dma((2,)), dma((2,)), dma((2,)), dma((2,)),
        dma((2,)), dma((2,)), dma((4, 2, 2)), dma((4, 2, 2)),
        dma((8,)), dma((8,)), dma((8,)), dma((8,)),
        dma((2, 4)), dma((2, 4)), dma((2, 4)), dma((2, 4)),
        dma((3, 8)), dma((3, 8)), dma((8,)), dma((8,)), dma((1,)), dma((1,)), dma((1,)),
    ]
    hbm = pl.BlockSpec(memory_space=pl.ANY)
    smem = pl.BlockSpec(memory_space=pltpu.SMEM)
    vmem = pl.BlockSpec(memory_space=pltpu.VMEM)
    return pl.pallas_call(
        kernel,
        out_shape=(
            jax.ShapeDtypeStruct((2, 64, 640), BF16),
            jax.ShapeDtypeStruct((2, 1024, 256), BF16),
            jax.ShapeDtypeStruct((64, 640), BF16),
        ),
        in_specs=[hbm] * 7 + [smem] * 4,
        out_specs=(vmem, hbm, vmem),
        scratch_shapes=scratch,
        compiler_params=pltpu.CompilerParams(
            collective_id=0, has_side_effects=True, vmem_limit_bytes=60 * 2**20
        ),
        cost_estimate=pl.CostEstimate(
            flops=40_000_000_000, bytes_accessed=24 * 2**20, transcendentals=36_000_000
        ),
        name="attend_and_project",
    )(*operands)


def shards(
    prefill_queries,
    span_kv,
    prefix_cache,
    span_offsets,
    prompt_lengths,
    decode_owner,
    out_weight,
    step_queries,
    step_kv,
    decode_cache,
    contexts,
):
    prefill_out, landed, decode_out = run_kernel(
        prefill_queries,
        span_kv.reshape(2, 64, 256),
        prefix_cache.reshape(2, 2048, 256),
        out_weight,
        step_queries,
        step_kv.reshape(4, 16, 256),
        decode_cache.reshape(16, 1024, 256),
        span_offsets,
        prompt_lengths,
        decode_owner,
        contexts,
    )
    prefill_out, landed, decode_out = hand_over(prefill_out, landed, decode_out)
    return (prefill_out, landed.reshape(2, 1024, 1, 256), decode_out.reshape(4, 16, 640))


def solution(mesh):
    placed = (
        P(None, "seq", ("head", "section")),
        P(None, "seq", ("head", "section"), None),
        P(None, "seq", ("head", "section"), None),
        P(),
        P(),
        P(),
        P(("head", "section"), None),
        P(None, "seq", ("head", "section")),
        P(None, "seq", ("head", "section"), None),
        P("seq", None, ("head", "section"), None),
        P("seq"),
    )
    return jax.shard_map(
        shards,
        mesh=mesh,
        in_specs=placed,
        out_specs=(
            P(None, "seq", ("head", "section")),
            P("seq", None, ("head", "section"), None),
            P(None, "seq", ("head", "section")),
        ),
        check_vma=False,
    )
```
